256 devices in a mesh: particle: 32 (over x, z), token: 8 (over y, core).
Axes of the slice: x: 4, y: 4, z: 8, core: 2. Of those that a mesh axis runs over, the one named last changes fastest.
Arguments:
- states: bfloat16 [64, 512, 768], P('particle', 'token'), may hold values from -6 to 6
- ancestors: int32 [64], P('particle'), may hold values from 0 to 63, as said below
- pair_bias: bfloat16 [16, 512, 512], P(None, 'token'), may hold values from -3 to 300, as said below
- key_mask: int32 [512], replicated, may hold values from 0 to 1, as said below
- gain_attn: float32 [768], replicated, may hold values from 0.1 to 1.9
- w_qkv: bfloat16 [768, 2304], replicated, may hold values from -0.21875 to 0.21875
- w_o: bfloat16 [768, 768], replicated, may hold values from -0.21875 to 0.21875
- gain_ff: float32 [768], replicated, may hold values from 0.1 to 1.9
- w_in: bfloat16 [2, 768, 1536], P(None, 'particle'), may hold values from -0.21875 to 0.21875
- w_out: bfloat16 [768, 1536], P('particle'), may hold values from -0.15625 to 0.15625
Outputs:
- new_states: bfloat16 [64, 512, 768], P('particle', 'token')
The draws below stay inside these ranges and needn't reach their ends.
Inputs may be any that keep to these rules, and one draw needn't show every extreme that they name: `ancestors`: any particle may be the ancestor of any number of particles. `pair_bias`: real values; rows of some heads may hold a few large entries. `key_mask`: 1 on a prefix of 256 or more tokens and 0 after it; the last token is always 0.
All inputs are finite; a program needn't handle non-finite values.
Results may differ from the reference program's by a relative error of at most 0.0085.
Values may be sent and summed in bfloat16 or wider, within the bound.
No kernel may reach another device: no remote copies, remote signals or barrier semaphores. Data moves between devices by JAX's collectives and lax.ppermute only.
A program may use at most 64 MiB of HBM per device.

```python
import math
import jax
import jax.numpy as jnp
from jax import lax

D = 768
HEADS = 16
FF = 1536
PART_DEV = 2
LEN = 512
PARTICLES = 64


def draw_ancestors(key, part):
    key = jax.random.fold_in(key, 7)
    key_prev, key_common, key_which, key_any, key_coin = jax.random.split(key, 5)
    index = jnp.arange(PARTICLES, dtype=jnp.int32)
    groups = PARTICLES // PART_DEV
    device = index // PART_DEV
    previous = (device - 1) % groups * PART_DEV + jax.random.randint(key_prev, (PARTICLES,), 0, PART_DEV)
    previous = jnp.where(index == 0, PARTICLES - 1, previous)
    previous = jnp.where(index == PART_DEV, 0, previous)
    common = jax.random.randint(key_common, (4,), 0, PARTICLES)
    common_pick = common[jax.random.randint(key_which, (PARTICLES,), 0, 4)]
    anywhere = jax.random.randint(key_any, (PARTICLES,), 0, PARTICLES)
    coin = jax.random.randint(key_coin, (PARTICLES,), 0, 2)
    other = jnp.where(coin == 0, common_pick, anywhere)
    return jnp.where(index % PART_DEV == 0, previous, other).astype(jnp.int32)


def draw_pair_bias(key, part):
    key = jax.random.fold_in(key, 11)
    key_base = jax.random.fold_in(key, 0)
    base = jnp.clip(jax.random.normal(key_base, (HEADS, LEN, LEN), jnp.float32), -3.0, 3.0)
    return base.astype(jnp.bfloat16)


def draw_key_mask(key, part):
    key = jax.random.fold_in(key, 5)
    length = jax.random.randint(key, (), LEN // 2, LEN)
    return (jnp.arange(LEN) < length).astype(jnp.int32)


def levels(rng, dims, shards, least, top_value):
    level = 1.0
    for position, blocks in shards:
        heights = jax.random.uniform(jax.random.fold_in(jax.random.fold_in(rng, 6), position), (blocks,), jnp.float32, least / len(shards), top_value / len(shards))
        level = level * jnp.repeat(jnp.exp(heights), dims[position] // blocks).reshape((-1,) + (1,) * (len(dims) - 1 - position))
    return level


def normal_values(stream_key, shape, spread, bound, shards=(), kind=jnp.bfloat16):
    entries = jax.random.normal(stream_key, shape, jnp.float32) * spread
    if len(shards) > 0:
        entries = levels(stream_key, shape, shards, -0.22, 0.18) * entries
    return jnp.clip(entries, min=-bound, max=bound).astype(kind)


def setup_inputs(seed: int = 0) -> dict:
    seeds = jax.random.split(jax.random.key(seed), 11)
    states = normal_values(seeds[0], (PARTICLES, LEN, D), 1.0, 6.0, ((0, 32), (1, 8)))
    ancestors = draw_ancestors(jax.random.fold_in(seeds[10], 71), 0)
    pair_bias = draw_pair_bias(jax.random.fold_in(seeds[10], 71), 0)
    key_mask = draw_key_mask(jax.random.fold_in(seeds[10], 71), 0)
    gain_attn = jnp.clip(1.0 + 0.18 * jax.random.normal(seeds[4], (D,), jnp.float32), 0.1, 1.9)
    w_qkv = normal_values(seeds[5], (D, 3 * D), D ** -0.5, 0.21875)
    w_o = normal_values(seeds[6], (D, D), D ** -0.5, 0.21875)
    gain_ff = jnp.clip(1.0 + 0.18 * jax.random.normal(seeds[7], (D,), jnp.float32), 0.1, 1.9)
    w_in = normal_values(seeds[8], (2, D, FF), D ** -0.5, 0.21875, ((1, 32),))
    w_out = normal_values(seeds[9], (D, FF), FF ** -0.5, 0.15625, ((0, 32),))
    return dict(states=states, ancestors=ancestors, pair_bias=pair_bias, key_mask=key_mask, gain_attn=gain_attn, w_qkv=w_qkv, w_o=w_o, gain_ff=gain_ff, w_in=w_in, w_out=w_out)


def rms_norm(stream, gain_vec):
    return stream * lax.rsqrt(lax.optimization_barrier(jnp.mean(stream * stream, axis=-1, keepdims=True)) + 1e-05) * gain_vec

def one_particle(particle_state, pair_bias, key_mask, gain_attn, w_qkv, w_o, gain_ff, w_in, w_out):
    head_size = D // HEADS
    stream = particle_state.astype(jnp.float32)
    normed = rms_norm(stream, gain_attn).astype(jnp.bfloat16)
    projected = jnp.dot(normed, w_qkv, preferred_element_type=jnp.float32)
    queries = (projected[:, :D] * (1.0 / math.sqrt(head_size))).astype(jnp.bfloat16)
    keys = projected[:, D:2 * D].astype(jnp.bfloat16)
    values = projected[:, 2 * D:].astype(jnp.bfloat16)
    usable = (key_mask > 0)[None, :]
    query_heads = queries.reshape(LEN, HEADS, head_size).transpose(1, 0, 2)
    key_heads = keys.reshape(LEN, HEADS, head_size).transpose(1, 0, 2)
    value_heads = values.reshape(LEN, HEADS, head_size).transpose(1, 0, 2)

    def one_head(head_items):
        query_head, key_head, value_head, bias_head = head_items
        scores = jnp.dot(query_head, key_head.T, preferred_element_type=jnp.float32) + bias_head.astype(jnp.float32)
        row_max = lax.optimization_barrier(jnp.max(jnp.where(usable, scores, -1e+30), axis=1, keepdims=True))
        weights = jnp.where(usable, jnp.exp(scores - row_max), 0.0)
        row_total = lax.optimization_barrier(jnp.sum(weights, axis=1, keepdims=True))
        mixture = jnp.dot(weights.astype(jnp.bfloat16), value_head, preferred_element_type=jnp.float32)
        return mixture / row_total
    head_out = lax.map(one_head, (query_heads, key_heads, value_heads, pair_bias))
    attended = head_out.transpose(1, 0, 2).reshape(LEN, D).astype(jnp.bfloat16)
    stream = stream + jnp.dot(attended, w_o, preferred_element_type=jnp.float32)
    normed_ff = rms_norm(stream, gain_ff).astype(jnp.bfloat16)
    gate_term = jnp.dot(normed_ff, w_in[0], preferred_element_type=jnp.float32)
    up_term = jnp.dot(normed_ff, w_in[1], preferred_element_type=jnp.float32)
    hidden = (jax.nn.silu(gate_term) * up_term).astype(jnp.bfloat16)
    update = lax.dot_general(hidden, w_out, (((1,), (1,)), ((), ())), preferred_element_type=jnp.float32)
    return (stream + update).astype(jnp.bfloat16)

def reference(states, ancestors, pair_bias, key_mask, gain_attn, w_qkv, w_o, gain_ff, w_in, w_out):
    chosen = jnp.take(states, ancestors.astype(jnp.int32), axis=0)

    def run_one(particle_state):
        return one_particle(particle_state, pair_bias, key_mask, gain_attn, w_qkv, w_o, gain_ff, w_in, w_out)
    return lax.map(run_one, chosen)
```

```python
import functools
import math

import jax
import jax.numpy as jnp
from jax import lax
from jax.experimental import pallas as pl
from jax.experimental.pallas import tpu as pltpu
from jax.sharding import Mesh
from jax.sharding import PartitionSpec as P

NX, NZ, NY, NC = 4, 8, 4, 2
PARTICLE = ("x", "z")
HEADS = 16
EPS = 1e-05
VMEM = pl.BlockSpec(memory_space=pltpu.VMEM)
SMEM = pl.BlockSpec(memory_space=pltpu.SMEM)


def rms_norm(stream, gain_vec):
    return stream * lax.rsqrt(jnp.mean(stream * stream, axis=-1, keepdims=True) + EPS) * gain_vec


def attention_kernel(
    place, n0, n1, n2, n3, x, w_qkv, bias_own, bias_other, mask, w_o, gain_ff,
    stream_ref, normed_ff_ref, rows_all, keys, values, queries, attended,
):
    y, c = place[0], place[1]
    row_count, width = x.shape
    half = row_count // 2
    head_size = width // HEADS
    for k, block in enumerate((n0, n1, n2, n3)):
        at = pl.multiple_of(lax.rem(y + (NY - k), NY) * row_count, row_count)
        rows_all[pl.ds(at, row_count), :] = block[...]
    own = pl.multiple_of(c * half, half)
    other = pl.multiple_of((1 - c) * half, half)
    own_rows = jnp.concatenate([n0[pl.ds(own, half), :], n0[pl.ds(other, half), :]], axis=0)
    scale = 1.0 / math.sqrt(head_size)
    queries[...] = (
        jnp.dot(own_rows, w_qkv[:, :width], preferred_element_type=jnp.float32) * scale
    ).astype(jnp.bfloat16)
    step = 256
    for part, dest in ((1, keys), (2, values)):
        for at in range(0, width, step):
            dest[:, at : at + step] = jnp.dot(
                rows_all[...],
                w_qkv[:, part * width + at : part * width + at + step],
                preferred_element_type=jnp.float32,
            ).astype(jnp.bfloat16)
    unusable = jnp.where(mask[...] > 0, 0.0, -1e30)
    attended[...] = jnp.zeros_like(attended)
    for h in range(HEADS):
        first, last = h * head_size, (h + 1) * head_size
        lo, hi = first // 128 * 128, -(-last // 128) * 128
        lanes = lax.broadcasted_iota(jnp.int32, (1, hi - lo), 1) + lo
        inside = (lanes >= first) & (lanes < last)
        query_head = jnp.where(inside, queries[:, lo:hi], jnp.zeros((), jnp.bfloat16))
        scores = lax.dot_general(
            query_head, keys[:, lo:hi], (((1,), (1,)), ((), ())), preferred_element_type=jnp.float32
        )
        bias = jnp.concatenate([bias_own[h], bias_other[h]], axis=0).astype(jnp.float32)
        scores = scores + bias + unusable
        weights = jnp.exp(scores - jnp.max(scores, axis=1, keepdims=True))
        total = jnp.sum(weights, axis=1, keepdims=True)
        mixture = jnp.dot(
            weights.astype(jnp.bfloat16), values[:, lo:hi], preferred_element_type=jnp.float32
        )
        attended[:, lo:hi] += jnp.where(inside, mixture / total, 0.0)
    x_rows = jnp.concatenate([x[pl.ds(own, half), :], x[pl.ds(other, half), :]], axis=0)
    stream = x_rows.astype(jnp.float32) + jnp.dot(
        attended[...].astype(jnp.bfloat16), w_o[...], preferred_element_type=jnp.float32
    )
    stream_ref[...] = stream
    normed_ff_ref[...] = rms_norm(stream, gain_ff[...]).astype(jnp.bfloat16)


def transition_kernel(place, own, other, stream, weights, keep_ref, send_ref):
    c = place[1]
    half = own.shape[0] // 2
    rows = jnp.concatenate([own[...], other[...]], axis=0)
    gate = jnp.dot(rows, weights[0], preferred_element_type=jnp.float32)
    up = jnp.dot(rows, weights[1], preferred_element_type=jnp.float32)
    hidden = (gate / (1.0 + jnp.exp(-gate)) * up).astype(jnp.bfloat16)
    update = lax.dot_general(
        hidden, weights[2], (((1,), (1,)), ((), ())), preferred_element_type=jnp.float32
    )
    keep_ref[c] = update[:half] + stream[:half]
    send_ref[c] = update[half : 2 * half] + stream[half:]
    send_ref[1 - c] = update[2 * half : 3 * half]
    keep_ref[1 - c] = update[3 * half :]


def swap_cores(value):
    return lax.ppermute(value, "c", [(0, 1), (1, 0)])


def body(states, ancestors, pair_bias, key_mask, gain_attn, w_qkv, w_o, gain_ff, w_in, w_out):
    part_count, block_rows, width = states.shape
    groups = NX * NZ
    each = block_rows // groups
    rows = block_rows * NC
    c = lax.axis_index("c")
    place = jnp.stack([lax.axis_index("y"), c]).astype(jnp.int32)

    hidden_half = w_out.shape[1] // NC
    local = jnp.concatenate([w_in, w_out[None]], axis=0)
    local = lax.dynamic_slice_in_dim(local, c * hidden_half, hidden_half, axis=2)
    ff_weights = lax.all_gather(local, PARTICLE, axis=1, tiled=True)
    bias_other = swap_cores(pair_bias)

    spread = states.reshape(part_count, groups, each, width).transpose(1, 0, 2, 3)
    names = jnp.broadcast_to(
        ancestors.astype(jnp.bfloat16)[None, :, None, None], (groups, part_count, each, 128)
    )
    spread = jnp.concatenate([spread, names], axis=3).reshape(groups, part_count * each, width + 128)
    spread = lax.all_to_all(spread, PARTICLE, 0, 0)
    wanted = spread[:, ::each, width].astype(jnp.int32).T.reshape(-1)
    source = lax.iota(jnp.int32, groups * part_count)
    onehot = (wanted[:, None] == source[None, :]).astype(jnp.bfloat16)
    picked = jnp.einsum(
        "ds,sre->dre",
        onehot,
        spread[:, :, :width].reshape(groups * part_count, each, width),
        preferred_element_type=jnp.float32,
    ).astype(jnp.bfloat16)
    chosen = lax.all_to_all(picked, ("c",) + PARTICLE, 0, 0).reshape(rows, width)

    normed = rms_norm(chosen.astype(jnp.float32), gain_attn).astype(jnp.bfloat16)
    blocks = [normed] + [
        lax.ppermute(normed, "y", [(i, (i + k) % NY) for i in range(NY)]) for k in range(1, NY)
    ]
    stream, normed_ff = pl.pallas_call(
        attention_kernel,
        out_shape=(
            jax.ShapeDtypeStruct((rows, width), jnp.float32),
            jax.ShapeDtypeStruct((rows, width), jnp.bfloat16),
        ),
        in_specs=[SMEM] + [VMEM] * 11,
        out_specs=(VMEM, VMEM),
        scratch_shapes=[
            pltpu.VMEM((rows * NY, width), jnp.bfloat16),
            pltpu.VMEM((rows * NY, width), jnp.bfloat16),
            pltpu.VMEM((rows * NY, width), jnp.bfloat16),
            pltpu.VMEM((rows, width), jnp.bfloat16),
            pltpu.VMEM((rows, width), jnp.float32),
        ],
        compiler_params=pltpu.CompilerParams(vmem_limit_bytes=32 * 2**20),
        name="attention",
    )(
        place, *blocks, chosen, w_qkv, pair_bias, bias_other, key_mask[None], w_o, gain_ff[None]
    )
    keep, send = pl.pallas_call(
        transition_kernel,
        out_shape=(jax.ShapeDtypeStruct((part_count, block_rows, width), jnp.float32),) * 2,
        in_specs=[SMEM] + [VMEM] * 4,
        out_specs=(VMEM, VMEM),
        compiler_params=pltpu.CompilerParams(vmem_limit_bytes=32 * 2**20),
        name="transition",
    )(place, normed_ff, swap_cores(normed_ff), stream, ff_weights)
    return (keep + swap_cores(send)).astype(jnp.bfloat16)


def solution(mesh):
    fine = Mesh(mesh.devices.reshape(NX, NZ, NY, NC), ("x", "z", "y", "c"))
    token = ("y", "c")
    placed = (
        P(PARTICLE, token, None),
        P(PARTICLE),
        P(None, token, None),
        P(),
        P(),
        P(),
        P(),
        P(),
        P(None, PARTICLE, None),
        P(PARTICLE, None),
    )
    return jax.shard_map(
        body, mesh=fine, in_specs=placed, out_specs=P(PARTICLE, token, None), check_vma=False
    )
```

```python
import math

import jax
import jax.numpy as jnp
import numpy as np
from jax import lax
from jax.experimental import pallas as pl
from jax.experimental.pallas import tpu as pltpu
from jax.sharding import Mesh
from jax.sharding import PartitionSpec as P

NX, NZ, NY, NC = 4, 8, 4, 2
GROUP = NX * NZ
PARTICLE = ("x", "z")
HEADS = 16
EPS = 1e-05
PIECE = 4
TILE = 8
TILES = 8
MIB = 2**20
ANY = pl.BlockSpec(memory_space=pl.ANY)
VMEM = pl.BlockSpec(memory_space=pltpu.VMEM)
SMEM = pl.BlockSpec(memory_space=pltpu.SMEM)


def rms_norm(stream, gain_vec):
    return stream * lax.rsqrt(jnp.mean(stream * stream, axis=-1, keepdims=True) + EPS) * gain_vec


def iotas(shape):
    return lax.broadcasted_iota(jnp.int32, shape, 0), lax.broadcasted_iota(jnp.int32, shape, 1)


def reorder(onehot, values):
    return jnp.dot(onehot.astype(jnp.bfloat16), values, preferred_element_type=jnp.float32)


def weight_orders(width):
    depth = width // GROUP
    tile, source, row = np.meshgrid(np.arange(3), np.arange(GROUP), np.arange(TILE), indexing="ij")
    inputs = (source * depth + tile * TILE + row).reshape(-1)
    outputs = np.concatenate([inputs[: 2 * GROUP * TILE], inputs[2 * GROUP * TILE :].reshape(GROUP, TILE).T.reshape(-1)])
    eye = np.eye(width, dtype=jnp.bfloat16)
    return eye[:, inputs], eye[outputs]


def spread_kernel(place, ancestors, states, w_in, w_out, out_ref, local):
    y, c = place[0], place[1]
    part_count, rows, width = states.shape
    half = width // 2
    both = 2 * PIECE
    out_row, in_row = iotas((part_count * rows, part_count * rows))
    group, part, row = out_row // both, out_row // PIECE % 2, out_row % PIECE
    onehot = in_row == part * rows + group * PIECE + row
    moved = reorder(onehot, states[...].reshape(part_count * rows, width))
    for h in range(2):
        out_ref[:, h, :, :half] = (
            moved[:, h * half : (h + 1) * half].reshape(-1, both, half).astype(jnp.bfloat16)
        )
    depth = w_out.shape[0]
    mine = pl.ds(pl.multiple_of(c * width, 128), width)
    local[: 2 * depth] = w_in[:, :, mine].astype(jnp.float32).reshape(2 * depth, width)
    local[2 * depth :] = w_out[:, mine].astype(jnp.float32)
    lanes = pl.ds(pl.multiple_of(lax.rem(y, 2) * half, 128), half)
    tile_row = lax.broadcasted_iota(jnp.int32, (both, 128), 0)
    names = jnp.where(tile_row == 3, ancestors[0], ancestors[1]).astype(jnp.float32)
    groups = GROUP // NX // 2
    for x in range(NX):
        e = 2 * x + y // 2
        tile = local[pl.ds(pl.multiple_of(e * TILE, TILE), TILE), lanes]
        extra = local[pl.ds(TILES * TILE + e, 1), lanes]
        last = names
        for i in range(3):
            last = jnp.where(tile_row == i, extra[:, i * 128 : (i + 1) * 128], last)
        at = slice(x * groups, (x + 1) * groups)
        shape = (groups, 2, both)
        out_ref[at, :, :, half:width] = jnp.broadcast_to(tile.astype(jnp.bfloat16), shape + (half,))
        out_ref[at, :, :, width:] = jnp.broadcast_to(last.astype(jnp.bfloat16), shape + (128,))


def pick_kernel(place, pieces, picked_ref, weights_ref):
    c = place[1]
    half = picked_ref.shape[2]
    width = 2 * half
    rows = pieces[...].astype(jnp.float32).reshape(-1, width + 128)
    count = rows.shape[0]
    last = rows[:, width:].astype(jnp.bfloat16)
    out_row, in_row = iotas((count, count))
    part = lax.rem(out_row // PIECE + c, 2)
    names = reorder(in_row == out_row // TILE * TILE + 3 + part, last)[:, :1]
    onehot = in_row == names.astype(jnp.int32) * PIECE + out_row % PIECE
    picked = reorder(onehot, rows[:, :half].astype(jnp.bfloat16))
    picked_ref[...] = picked.reshape(picked_ref.shape).astype(jnp.bfloat16)
    weights_ref[:count] = rows[:, half:width].astype(jnp.bfloat16)
    out_row, in_row = iotas((GROUP, count))
    for i in range(3):
        extra = reorder(in_row == out_row * TILE + i, last).astype(jnp.bfloat16)
        weights_ref[count:, i * 128 : (i + 1) * 128] = extra


def column_kernel(place, w0, w1, w2, w3, out_ref):
    half = w0.shape[1]
    for k, block in enumerate((w0, w1, w2, w3)):
        y = lax.rem(place[0] + (NY - k), NY)
        lanes = pl.ds(pl.multiple_of(lax.rem(y, 2) * half, 128), half)
        out_ref[y // 2, :, lanes] = block[...]


def rows_kernel(pieces, keep_ref, send_ref):
    rows, width = keep_ref.shape
    half = width // 2
    both = 2 * PIECE
    out_row, in_row = iotas((2 * rows, 2 * rows))
    part, at = out_row // rows, out_row % rows
    onehot = in_row == at // PIECE * both + part * PIECE + at % PIECE
    for h in range(2):
        values = pieces[:, h].astype(jnp.float32).reshape(2 * rows, half).astype(jnp.bfloat16)
        moved = reorder(onehot, values).astype(jnp.bfloat16)
        keep_ref[:, h * half : (h + 1) * half] = moved[:rows]
        send_ref[:, h * half : (h + 1) * half] = moved[rows:]


def norm_kernel(place, own, other, gain, normed_ref):
    c = place[1]
    rows = own.shape[0]
    for values, slot in ((own, c), (other, 1 - c)):
        at = pl.ds(pl.multiple_of(slot * rows, rows), rows)
        normed = rms_norm(values[...].astype(jnp.float32), gain[...][None, :])
        normed_ref[at, :] = normed.astype(jnp.bfloat16)


def project_kernel(place, normed, w_qkv, queries_ref, keys_ref, values_ref):
    c = place[1]
    row_count, width = normed.shape
    half = row_count // 2
    scale = 1.0 / math.sqrt(width // HEADS)
    projected = jnp.dot(normed[...], w_qkv[...], preferred_element_type=jnp.float32)
    queries = (projected[:, :width] * scale).astype(jnp.bfloat16)
    for slot, at in ((c, 0), (1 - c, half)):
        queries_ref[pl.ds(pl.multiple_of(slot * half, half), half), :] = queries[at : at + half]
    keys_ref[...] = projected[:, width : 2 * width].astype(jnp.bfloat16)
    values_ref[...] = projected[:, 2 * width :].astype(jnp.bfloat16)


def attention_kernel(
    place, n1, n2, n3, queries, key_own, value_own, x_own, x_other, w_qkv, bias_own, bias_other,
    mask, w_o, gain_ff, order, stream_ref, normed_ff_ref,
    rows_all, keys, values, attended, bias, w_o_here, order_here, arrived, loaded,
):
    y = place[0]
    row_count, width = queries.shape
    half = row_count // 2
    head_size = width // HEADS
    blocks = [
        pltpu.make_async_copy(block, rows_all.at[pl.ds(k * row_count, row_count)], arrived.at[k])
        for k, block in enumerate((n1, n2, n3))
    ]
    loads = [
        pltpu.make_async_copy(bias_own, bias.at[:, :half], loaded.at[0]),
        pltpu.make_async_copy(bias_other, bias.at[:, half:], loaded.at[1]),
        pltpu.make_async_copy(w_o, w_o_here, loaded.at[2]),
        pltpu.make_async_copy(order, order_here, loaded.at[3]),
    ]
    for copy in blocks + loads:
        copy.start()
    spots = [
        pl.ds(pl.multiple_of(lax.rem(y + (NY - k), NY) * row_count, row_count), row_count)
        for k in range(NY)
    ]
    keys[spots[0], :] = key_own[...]
    values[spots[0], :] = value_own[...]
    for copy in blocks:
        copy.wait()
    step = 256
    for part, dest in ((1, keys), (2, values)):
        for at in range(0, width, step):
            made = jnp.dot(
                rows_all[...],
                w_qkv[:, part * width + at : part * width + at + step],
                preferred_element_type=jnp.float32,
            ).astype(jnp.bfloat16)
            for k in range(1, NY):
                dest[spots[k], at : at + step] = made[(k - 1) * row_count : k * row_count]
    unusable = jnp.where(mask[...][None, :] > 0, 0.0, -1e30)
    attended[...] = jnp.zeros_like(attended)
    for copy in loads[:2]:
        copy.wait()
    for h in range(HEADS):
        first, last = h * head_size, (h + 1) * head_size
        lo, hi = first // 128 * 128, -(-last // 128) * 128
        lanes = lax.broadcasted_iota(jnp.int32, (1, hi - lo), 1) + lo
        inside = (lanes >= first) & (lanes < last)
        query_head = jnp.where(inside, queries[:, lo:hi], jnp.zeros((), jnp.bfloat16))
        scores = lax.dot_general(
            query_head, keys[:, lo:hi], (((1,), (1,)), ((), ())), preferred_element_type=jnp.float32
        )
        scores = scores + bias[h].astype(jnp.float32) + unusable
        weights = jnp.exp(scores - jnp.max(scores, axis=1, keepdims=True))
        total = jnp.sum(weights, axis=1, keepdims=True)
        mixture = jnp.dot(
            weights.astype(jnp.bfloat16), values[:, lo:hi], preferred_element_type=jnp.float32
        )
        attended[:, lo:hi] += jnp.where(inside, mixture / total, 0.0)
    x_rows = jnp.concatenate([x_own[...], x_other[...]], axis=0)
    for copy in loads[2:]:
        copy.wait()
    stream = x_rows.astype(jnp.float32) + jnp.dot(
        attended[...].astype(jnp.bfloat16), w_o_here[...], preferred_element_type=jnp.float32
    )
    stream_ref[...] = stream
    normed_ff = rms_norm(stream, gain_ff[...][None, :]).astype(jnp.bfloat16)
    normed_ff_ref[...] = jnp.dot(
        normed_ff, order_here[...], preferred_element_type=jnp.float32
    ).astype(jnp.bfloat16)


def transition_kernel(
    place, own, other, stream, order, w0, w1, w2, w3, keep_ref, send_ref, tiles, extras, arrived
):
    c, x = place[1], place[2]
    half = own.shape[0] // 2
    width = own.shape[1]
    count = tiles.shape[1]
    copies = []
    for k, block in enumerate((w0, w1, w2, w3)):
        at = pl.ds(lax.rem(x + (NX - k), NX) * 2, 2)
        copies.append(pltpu.make_async_copy(block.at[:, :count], tiles.at[at], arrived.at[2 * k]))
        copies.append(pltpu.make_async_copy(block.at[:, count:], extras.at[at], arrived.at[2 * k + 1]))
    for copy in copies:
        copy.start()
    rows = jnp.concatenate([own[...], other[...]], axis=0)
    for copy in copies:
        copy.wait()
    gate = jnp.dot(rows, tiles[0:3].reshape(width, width), preferred_element_type=jnp.float32)
    up = jnp.dot(rows, tiles[3:6].reshape(width, width), preferred_element_type=jnp.float32)
    hidden = (gate / (1.0 + jnp.exp(-gate)) * up).astype(jnp.bfloat16)
    across = (((1,), (1,)), ((), ()))
    update = jnp.concatenate(
        [
            lax.dot_general(
                hidden, tiles[6:8].reshape(2 * count, width), across, preferred_element_type=jnp.float32
            ),
            lax.dot_general(
                hidden, extras[...].reshape(-1, width), across, preferred_element_type=jnp.float32
            ),
        ],
        axis=1,
    )
    high = update.astype(jnp.bfloat16)
    low = (update - high.astype(jnp.float32)).astype(jnp.bfloat16)
    update = jnp.dot(high, order[...], preferred_element_type=jnp.float32) + jnp.dot(
        low, order[...], preferred_element_type=jnp.float32
    )
    keep_ref[c] = update[:half] + stream[:half]
    send_ref[c] = update[half : 2 * half] + stream[half:]
    send_ref[1 - c] = update[2 * half : 3 * half]
    keep_ref[1 - c] = update[3 * half :]


def swap_cores(value):
    return lax.ppermute(value, "c", [(0, 1), (1, 0)])


def others(value, axis, size):
    return [
        lax.ppermute(value, axis, [(i, (i + k) % size) for i in range(size)]) for k in range(1, size)
    ]


def kernel(f, name, specs, args, shapes, limit=8, scratch=()):
    def whole(shape):
        return pl.BlockSpec(shape, lambda i: (0,) * len(shape))

    specs = [whole(a.shape) if s is None else s for s, a in zip(specs, args, strict=True)]
    outs = tuple(jax.ShapeDtypeStruct(shape, dtype) for shape, dtype in shapes)
    return pl.pallas_call(
        f,
        grid=(1,),
        out_shape=outs,
        in_specs=specs,
        out_specs=tuple(whole(o.shape) for o in outs),
        scratch_shapes=scratch,
        compiler_params=pltpu.CompilerParams(vmem_limit_bytes=limit * MIB),
        name=name,
    )(*args)


def body(states, ancestors, pair_bias, key_mask, gain_attn, w_qkv, w_o, gain_ff, w_in, w_out):
    part_count, block_rows, width = states.shape
    rows = block_rows * NC
    half = width // 2
    both = 2 * PIECE
    depth = w_out.shape[0]
    bf16, f32 = jnp.bfloat16, jnp.float32
    place = jnp.stack([lax.axis_index(a) for a in ("y", "c", "x")]).astype(jnp.int32)
    order_in, order_out = weight_orders(width)

    bias_other = swap_cores(pair_bias)
    (pieces,) = kernel(
        spread_kernel,
        "spread",
        [SMEM, SMEM, None, None, None],
        (place, ancestors, states, w_in, w_out),
        [((GROUP // 2, 2, both, width + 128), bf16)],
        scratch=[pltpu.VMEM((3 * depth, width), f32)],
    )
    pieces = lax.all_to_all(pieces.reshape(GROUP, both, width + 128), PARTICLE, 0, 0)
    picked, piece = kernel(
        pick_kernel,
        "pick",
        [SMEM, None],
        (place, pieces),
        [((GROUP, both, half), bf16), ((GROUP * (TILE + 1), half), bf16)],
    )
    ring = [piece] + others(piece, "y", NY)
    (column,) = kernel(
        column_kernel,
        "column",
        [SMEM] + [None] * NY,
        (place, *ring),
        [((2, GROUP * (TILE + 1), width), bf16)],
    )
    columns = [column] + others(column, "x", NX)
    picked = lax.all_to_all(picked, PARTICLE, 0, 0)
    x_own, x_send = kernel(
        rows_kernel,
        "rows",
        [None],
        (picked.reshape(GROUP // 2, 2, both, half),),
        [((block_rows, width), bf16)] * 2,
    )
    x_other = swap_cores(x_send)
    (normed,) = kernel(
        norm_kernel,
        "norm",
        [SMEM, None, None, None],
        (place, x_own, x_other, gain_attn),
        [((rows, width), bf16)],
    )
    blocks = others(normed, "y", NY)
    queries, key_own, value_own = kernel(
        project_kernel,
        "project",
        [SMEM, None, VMEM],
        (place, normed, w_qkv),
        [((rows, width), bf16)] * 3,
    )
    stream, normed_ff = kernel(
        attention_kernel,
        "attention",
        [SMEM] + [ANY] * 3 + [None] * 5 + [VMEM, ANY, ANY, None, ANY, None, ANY],
        (
            place, *blocks, queries, key_own, value_own, x_own, x_other, w_qkv, pair_bias,
            bias_other, key_mask, w_o, gain_ff, order_in,
        ),
        [((rows, width), f32), ((rows, width), bf16)],
        limit=16,
        scratch=[
            pltpu.VMEM((rows * (NY - 1), width), bf16),
            pltpu.VMEM((rows * NY, width), bf16),
            pltpu.VMEM((rows * NY, width), bf16),
            pltpu.VMEM((rows, width), f32),
            pltpu.VMEM((HEADS, rows, rows * NY), bf16),
            pltpu.VMEM((width, width), bf16),
            pltpu.VMEM((width, width), bf16),
            pltpu.SemaphoreType.DMA((NY - 1,)),
            pltpu.SemaphoreType.DMA((4,)),
        ],
    )
    keep, send = kernel(
        transition_kernel,
        "transition",
        [SMEM, None, None, None, None] + [ANY] * NX,
        (place, normed_ff, swap_cores(normed_ff), stream, order_out, *columns),
        [((part_count, block_rows, width), f32)] * 2,
        limit=16,
        scratch=[
            pltpu.VMEM((TILES, GROUP * TILE, width), bf16),
            pltpu.VMEM((TILES, GROUP, width), bf16),
            pltpu.SemaphoreType.DMA((2 * NX,)),
        ],
    )
    return (keep + swap_cores(send)).astype(bf16)


def solution(mesh):
    fine = Mesh(mesh.devices.reshape(NX, NZ, NY, NC), ("x", "z", "y", "c"))
    token = ("y", "c")
    placed = (
        P(PARTICLE, token, None),
        P(PARTICLE),
        P(None, token, None),
        P(),
        P(),
        P(),
        P(),
        P(),
        P(None, PARTICLE, None),
        P(PARTICLE, None),
    )
    return jax.shard_map(
        body, mesh=fine, in_specs=placed, out_specs=P(PARTICLE, token, None), check_vma=False
    )
```

```python
import math

import jax
import jax.numpy as jnp
import numpy as np
from jax import lax
from jax.experimental import pallas as pl
from jax.experimental.pallas import tpu as pltpu
from jax.sharding import Mesh
from jax.sharding import PartitionSpec as P

NX, NZ, NY, NC = 4, 8, 4, 2
GROUP = NX * NZ
PARTICLE = ("x", "z")
HEADS = 16
EPS = 1e-05
PIECE = 4
TILE = 8
TILES = 8
MIB = 2**20
MICROSECOND = 10**9
ANY = pl.BlockSpec(memory_space=pl.ANY)
VMEM = pl.BlockSpec(memory_space=pltpu.VMEM)
SMEM = pl.BlockSpec(memory_space=pltpu.SMEM)


def rms_norm(stream, gain_vec):
    return stream * lax.rsqrt(jnp.mean(stream * stream, axis=-1, keepdims=True) + EPS) * gain_vec


def iotas(shape):
    return lax.broadcasted_iota(jnp.int32, shape, 0), lax.broadcasted_iota(jnp.int32, shape, 1)


def reorder(onehot, values):
    return jnp.dot(onehot.astype(jnp.bfloat16), values, preferred_element_type=jnp.float32)


def weight_orders(width):
    depth = width // GROUP
    tile, source, row = np.meshgrid(np.arange(3), np.arange(GROUP), np.arange(TILE), indexing="ij")
    inputs = (source * depth + tile * TILE + row).reshape(-1)
    outputs = np.concatenate([inputs[: 2 * GROUP * TILE], inputs[2 * GROUP * TILE :].reshape(GROUP, TILE).T.reshape(-1)])
    eye = np.eye(width, dtype=jnp.bfloat16)
    return eye[:, inputs], eye[outputs]


def spread_kernel(ancestors, states, w_in, w_out, out_ref, local):
    y, c = lax.axis_index("y"), lax.axis_index("c")
    part_count, rows, width = states.shape
    half = width // 2
    both = 2 * PIECE
    out_row, in_row = iotas((part_count * rows, part_count * rows))
    group, part, row = out_row // both, out_row // PIECE % 2, out_row % PIECE
    onehot = in_row == part * rows + group * PIECE + row
    moved = reorder(onehot, states[...].reshape(part_count * rows, width))
    for h in range(2):
        out_ref[:, h, :, :half] = (
            moved[:, h * half : (h + 1) * half].reshape(-1, both, half).astype(jnp.bfloat16)
        )
    depth = w_out.shape[0]
    mine = pl.ds(pl.multiple_of(c * width, 128), width)
    local[: 2 * depth] = w_in[:, :, mine].astype(jnp.float32).reshape(2 * depth, width)
    local[2 * depth :] = w_out[:, mine].astype(jnp.float32)
    lanes = pl.ds(pl.multiple_of(lax.rem(y, 2) * half, 128), half)
    tile_row = lax.broadcasted_iota(jnp.int32, (both, 128), 0)
    names = jnp.where(tile_row == 3, ancestors[0], ancestors[1]).astype(jnp.float32)
    groups = GROUP // NX // 2
    for x in range(NX):
        e = 2 * x + y // 2
        tile = local[pl.ds(pl.multiple_of(e * TILE, TILE), TILE), lanes]
        extra = local[pl.ds(TILES * TILE + e, 1), lanes]
        last = names
        for i in range(3):
            last = jnp.where(tile_row == i, extra[:, i * 128 : (i + 1) * 128], last)
        at = slice(x * groups, (x + 1) * groups)
        shape = (groups, 2, both)
        out_ref[at, :, :, half:width] = jnp.broadcast_to(tile.astype(jnp.bfloat16), shape + (half,))
        out_ref[at, :, :, width:] = jnp.broadcast_to(last.astype(jnp.bfloat16), shape + (128,))


def pick_kernel(pieces, picked_ref, weights_ref):
    c = lax.axis_index("c")
    half = picked_ref.shape[2]
    width = 2 * half
    rows = pieces[...].astype(jnp.float32).reshape(-1, width + 128)
    count = rows.shape[0]
    last = rows[:, width:].astype(jnp.bfloat16)
    out_row, in_row = iotas((count, count))
    part = lax.rem(out_row // PIECE + c, 2)
    names = reorder(in_row == out_row // TILE * TILE + 3 + part, last)[:, :1]
    onehot = in_row == names.astype(jnp.int32) * PIECE + out_row % PIECE
    picked = reorder(onehot, rows[:, :half].astype(jnp.bfloat16))
    picked_ref[...] = picked.reshape(picked_ref.shape).astype(jnp.bfloat16)
    weights_ref[:count] = rows[:, half:width].astype(jnp.bfloat16)
    out_row, in_row = iotas((GROUP, count))
    for i in range(3):
        extra = reorder(in_row == out_row * TILE + i, last).astype(jnp.bfloat16)
        weights_ref[count:, i * 128 : (i + 1) * 128] = extra


def column_kernel(w0, w1, w2, w3, out_ref):
    half = w0.shape[1]
    for k, block in enumerate((w0, w1, w2, w3)):
        y = lax.rem(lax.axis_index("y") + (NY - k), NY)
        lanes = pl.ds(pl.multiple_of(lax.rem(y, 2) * half, 128), half)
        out_ref[y // 2, :, lanes] = block[...]


def assemble(pieces, part, width):
    both = 2 * PIECE
    half = width // 2
    count = pieces.shape[0] // 2 * both
    out_row, in_row = iotas((count // 2, count))
    onehot = in_row == out_row // PIECE * both + part * PIECE + out_row % PIECE
    sides = []
    for h in range(2):
        values = pieces[:, :, :].reshape(-1, 2, both, half)[:, h]
        values = values.astype(jnp.float32).reshape(count, half).astype(jnp.bfloat16)
        sides.append(reorder(onehot, values))
    return jnp.concatenate(sides, axis=1)


def chip_rows(mine, theirs, width):
    return jnp.concatenate([assemble(mine, 0, width), assemble(theirs, 1, width)], axis=0)


def store_rows(ref, values):
    c = lax.axis_index("c")
    half = values.shape[0] // 2
    for slot, at in ((c, 0), (1 - c, half)):
        ref[pl.ds(pl.multiple_of(slot * half, half), half), :] = values[at : at + half].astype(ref.dtype)


def own_kernel(
    mine, theirs, gain, w_qkv, _bias, x_ref, normed_ref, queries_ref, keys_ref, values_ref
):
    width = x_ref.shape[1]
    rows = chip_rows(mine, theirs, width)
    x_ref[...] = rows.astype(jnp.bfloat16)
    normed = rms_norm(rows, gain[...][None, :])
    store_rows(normed_ref, normed)
    normed = normed.astype(jnp.bfloat16)
    projected = jnp.dot(normed, w_qkv[...], preferred_element_type=jnp.float32)
    scale = 1.0 / math.sqrt(width // HEADS)
    queries_ref[...] = (projected[:, :width] * scale).astype(jnp.bfloat16)
    store_rows(keys_ref, projected[:, width : 2 * width])
    store_rows(values_ref, projected[:, 2 * width :])


def other_kernel(normed, w_qkv, keys_ref, values_ref):
    width = keys_ref.shape[1]
    projected = jnp.dot(normed[...], w_qkv[:, width:], preferred_element_type=jnp.float32)
    keys_ref[...] = projected[:, :width].astype(jnp.bfloat16)
    values_ref[...] = projected[:, width:].astype(jnp.bfloat16)


def halves_kernel(left, right, _1, _2, _3, left_ref, right_ref, sent):
    copies = [
        pltpu.make_async_copy(left.at[:1], left_ref, sent.at[0]),
        pltpu.make_async_copy(right.at[1:], right_ref, sent.at[1]),
    ]
    for copy in copies:
        copy.start()
    for copy in copies:
        copy.wait()


def attention_kernel(
    k0, k1, k2, k3, v0, v1, v2, v3, queries, x_rows, bias_own, bias_other, mask, w_o, gain_ff, order,
    _left, _right, stream_ref, normed_ff_ref, keys, values, attended, bias, w_o_here, order_here, loaded,
):
    y = lax.axis_index("y")
    row_count, width = queries.shape
    half = row_count // 2
    head_size = width // HEADS
    loads = [
        pltpu.make_async_copy(bias_own, bias.at[:, :half], loaded.at[0]),
        pltpu.make_async_copy(bias_other, bias.at[:, half:], loaded.at[1]),
        pltpu.make_async_copy(w_o, w_o_here, loaded.at[2]),
        pltpu.make_async_copy(order, order_here, loaded.at[3]),
    ]
    for copy in loads:
        copy.start()
    for k, (key_block, value_block) in enumerate(((k0, v0), (k1, v1), (k2, v2), (k3, v3))):
        at = pl.multiple_of(lax.rem(y + (NY - k), NY) * row_count, row_count)
        keys[pl.ds(at, row_count), :] = key_block[...]
        values[pl.ds(at, row_count), :] = value_block[...]
    unusable = jnp.where(mask[...][None, :] > 0, 0.0, -1e30)
    attended[...] = jnp.zeros_like(attended)
    for copy in loads[:2]:
        copy.wait()
    together = 4
    for start in range(0, HEADS, together):
        heads = []
        for h in range(start, start + together):
            first, last = h * head_size, (h + 1) * head_size
            lo, hi = first // 128 * 128, -(-last // 128) * 128
            lanes = lax.broadcasted_iota(jnp.int32, (1, hi - lo), 1) + lo
            heads.append((h, lo, hi, (lanes >= first) & (lanes < last)))
        scores = [
            lax.dot_general(
                jnp.where(inside, queries[:, lo:hi], jnp.zeros((), jnp.bfloat16)),
                keys[:, lo:hi],
                (((1,), (1,)), ((), ())),
                preferred_element_type=jnp.float32,
            )
            for _, lo, hi, inside in heads
        ]
        weights, totals = [], []
        for (h, _, _, _), score in zip(heads, scores):
            score = score + bias[h].astype(jnp.float32) + unusable
            weight = jnp.exp(score - jnp.max(score, axis=1, keepdims=True))
            totals.append(jnp.sum(weight, axis=1, keepdims=True))
            weights.append(weight.astype(jnp.bfloat16))
        for (_, lo, hi, inside), weight, total in zip(heads, weights, totals):
            mixture = jnp.dot(weight, values[:, lo:hi], preferred_element_type=jnp.float32)
            attended[:, lo:hi] += jnp.where(inside, mixture / total, 0.0)
    for copy in loads[2:]:
        copy.wait()
    stream = x_rows[...].astype(jnp.float32) + jnp.dot(
        attended[...].astype(jnp.bfloat16), w_o_here[...], preferred_element_type=jnp.float32
    )
    stream_ref[...] = stream
    normed_ff = rms_norm(stream, gain_ff[...][None, :]).astype(jnp.bfloat16)
    normed_ff_ref[...] = jnp.dot(
        normed_ff, order_here[...], preferred_element_type=jnp.float32
    ).astype(jnp.bfloat16)


def transition_kernel(
    own, other, stream, order, here, left, right, far_0, far_1, keep_ref, send_ref,
    tiles, extras, arrived,
):
    c, x = lax.axis_index("c"), lax.axis_index("x")
    half = own.shape[0] // 2
    width = own.shape[1]
    count = tiles.shape[1]
    far = lax.rem(x + 2, NX) * 2
    parts = [
        (here, pl.ds(x * 2, 2)),
        (left, pl.ds(lax.rem(x + 3, NX) * 2, 2)),
        (right, pl.ds(lax.rem(x + 1, NX) * 2, 2)),
        (far_0, pl.ds(far, 1)),
        (far_1, pl.ds(far + 1, 1)),
    ]
    copies = []
    for k, (block, at) in enumerate(parts):
        copies.append(pltpu.make_async_copy(block.at[:, :count], tiles.at[at], arrived.at[2 * k]))
        copies.append(pltpu.make_async_copy(block.at[:, count:], extras.at[at], arrived.at[2 * k + 1]))
    for copy in copies:
        copy.start()
    rows = jnp.concatenate([own[...], other[...]], axis=0)
    for copy in copies:
        copy.wait()
    gate = jnp.dot(rows, tiles[0:3].reshape(width, width), preferred_element_type=jnp.float32)
    up = jnp.dot(rows, tiles[3:6].reshape(width, width), preferred_element_type=jnp.float32)
    hidden = (gate / (1.0 + jnp.exp(-gate)) * up).astype(jnp.bfloat16)
    across = (((1,), (1,)), ((), ()))
    update = jnp.concatenate(
        [
            lax.dot_general(
                hidden, tiles[6:8].reshape(2 * count, width), across, preferred_element_type=jnp.float32
            ),
            lax.dot_general(
                hidden, extras[...].reshape(-1, width), across, preferred_element_type=jnp.float32
            ),
        ],
        axis=1,
    )
    high = update.astype(jnp.bfloat16)
    low = (update - high.astype(jnp.float32)).astype(jnp.bfloat16)
    update = jnp.dot(high, order[...], preferred_element_type=jnp.float32) + jnp.dot(
        low, order[...], preferred_element_type=jnp.float32
    )
    keep_ref[c] = update[:half] + stream[:half]
    send_ref[c] = update[half : 2 * half] + stream[half:]
    send_ref[1 - c] = update[2 * half : 3 * half]
    keep_ref[1 - c] = update[3 * half :]


def swap_cores(value):
    return lax.ppermute(value, "c", [(0, 1), (1, 0)])


def others(value, axis, size):
    return [
        lax.ppermute(value, axis, [(i, (i + k) % size) for i in range(size)]) for k in range(1, size)
    ]


def kernel(f, name, specs, args, shapes, limit=8, scratch=(), out_spec=None, wait=1):
    def whole(shape):
        return pl.BlockSpec(shape, lambda i: (0,) * len(shape))

    specs = [whole(a.shape) if s is None else s for s, a in zip(specs, args, strict=True)]
    outs = tuple(jax.ShapeDtypeStruct(shape, dtype) for shape, dtype in shapes)
    return pl.pallas_call(
        f,
        grid=(1,),
        out_shape=outs,
        in_specs=specs,
        out_specs=tuple(out_spec or whole(o.shape) for o in outs),
        scratch_shapes=scratch,
        compiler_params=pltpu.CompilerParams(vmem_limit_bytes=limit * MIB),
        cost_estimate=pl.CostEstimate(
            flops=int(wait * MICROSECOND), bytes_accessed=0, transcendentals=0
        ),
        name=name,
    )(*args)


def body(states, ancestors, pair_bias, key_mask, gain_attn, w_qkv, w_o, gain_ff, w_in, w_out):
    part_count, block_rows, width = states.shape
    rows = block_rows * NC
    half = width // 2
    both = 2 * PIECE
    depth = w_out.shape[0]
    bf16, f32 = jnp.bfloat16, jnp.float32
    order_in, order_out = weight_orders(width)

    bias_other = swap_cores(pair_bias)
    (pieces,) = kernel(
        spread_kernel,
        "spread",
        [SMEM, None, None, None],
        (ancestors, states, w_in, w_out),
        [((GROUP // 2, 2, both, width + 128), bf16)],
        limit=56,
        scratch=[pltpu.VMEM((3 * depth, width), f32)],
    )
    pieces = lax.all_to_all(pieces.reshape(GROUP, both, width + 128), PARTICLE, 0, 0)
    picked, piece = kernel(
        pick_kernel,
        "pick",
        [None],
        (pieces,),
        [((GROUP, both, half), bf16), ((GROUP * (TILE + 1), half), bf16)],
        limit=56,
    )
    ring = [piece] + others(piece, "y", NY)
    (column,) = kernel(
        column_kernel,
        "column",
        [None] * NY,
        ring,
        [((2, GROUP * (TILE + 1), width), bf16)],
    )
    forward, back = ([(i, (i + k) % NX) for i in range(NX)] for k in (1, -1))
    left, right = lax.ppermute(column, "x", forward), lax.ppermute(column, "x", back)

    mine = lax.all_to_all(picked, PARTICLE, 0, 0)
    x_rows, normed, queries, *own = kernel(
        own_kernel,
        "own",
        [None, None, None, VMEM, ANY],
        (mine, swap_cores(mine), gain_attn, w_qkv, bias_other),
        [((rows, width), bf16)] * 5,
    )
    made = [own] + [
        kernel(other_kernel, "other", [None, VMEM], (block, w_qkv), [((rows, width), bf16)] * 2)
        for block in others(normed, "y", NY)
    ]
    left_half, right_half = kernel(
        halves_kernel,
        "halves",
        [ANY] * (2 + NY - 1),
        (left, right, *(k for k, _ in made[1:])),
        [((1,) + column.shape[1:], bf16)] * 2,
        out_spec=ANY,
        scratch=[pltpu.SemaphoreType.DMA((2,))],
    )
    far = [lax.ppermute(left_half, "x", forward), lax.ppermute(right_half, "x", back)]
    stream, normed_ff = kernel(
        attention_kernel,
        "attention",
        [None] * 10 + [ANY, ANY, None, ANY, None] + [ANY] * 3,
        (
            *[k for k, _ in made], *[v for _, v in made], queries, x_rows, pair_bias, bias_other,
            key_mask, w_o, gain_ff, order_in, left_half, right_half,
        ),
        [((rows, width), f32), ((rows, width), bf16)],
        limit=16,
        wait=4,
        scratch=[
            pltpu.VMEM((rows * NY, width), bf16),
            pltpu.VMEM((rows * NY, width), bf16),
            pltpu.VMEM((rows, width), f32),
            pltpu.VMEM((HEADS, rows, rows * NY), bf16),
            pltpu.VMEM((width, width), bf16),
            pltpu.VMEM((width, width), bf16),
            pltpu.SemaphoreType.DMA((4,)),
        ],
    )
    keep, send = kernel(
        transition_kernel,
        "transition",
        [None] * 4 + [ANY] * 5,
        (normed_ff, swap_cores(normed_ff), stream, order_out, column, left, right, *far),
        [((part_count, block_rows, width), f32)] * 2,
        limit=16,
        scratch=[
            pltpu.VMEM((TILES, GROUP * TILE, width), bf16),
            pltpu.VMEM((TILES, GROUP, width), bf16),
            pltpu.SemaphoreType.DMA((10,)),
        ],
    )
    return (keep + swap_cores(send)).astype(bf16)


def solution(mesh):
    fine = Mesh(mesh.devices.reshape(NX, NZ, NY, NC), ("x", "z", "y", "c"))
    token = ("y", "c")
    placed = (
        P(PARTICLE, token, None),
        P(PARTICLE),
        P(None, token, None),
        P(),
        P(),
        P(),
        P(),
        P(),
        P(None, PARTICLE, None),
        P(PARTICLE, None),
    )
    return jax.shard_map(
        body, mesh=fine, in_specs=placed, out_specs=P(PARTICLE, token, None), check_vma=False
    )
```

```python
import math

import jax
import jax.numpy as jnp
import numpy as np
from jax import lax
from jax.experimental import pallas as pl
from jax.experimental.pallas import tpu as pltpu
from jax.sharding import Mesh
from jax.sharding import PartitionSpec as P

NX, NZ, NY, NC = 4, 8, 4, 2
GROUP = NX * NZ
PARTICLE = ("x", "z")
HEADS = 16
EPS = 1e-05
PIECE = 4
TILE = 8
TILES = 8
MIB = 2**20
MICROSECOND = 10**9
ANY = pl.BlockSpec(memory_space=pl.ANY)
VMEM = pl.BlockSpec(memory_space=pltpu.VMEM)
SMEM = pl.BlockSpec(memory_space=pltpu.SMEM)


def rms_norm(stream, gain_vec):
    return stream * lax.rsqrt(jnp.mean(stream * stream, axis=-1, keepdims=True) + EPS) * gain_vec


def iotas(shape):
    return lax.broadcasted_iota(jnp.int32, shape, 0), lax.broadcasted_iota(jnp.int32, shape, 1)


def reorder(onehot, values):
    return jnp.dot(onehot.astype(jnp.bfloat16), values, preferred_element_type=jnp.float32)


def weight_orders(width):
    depth = width // GROUP
    tile, source, row = np.meshgrid(np.arange(3), np.arange(GROUP), np.arange(TILE), indexing="ij")
    inputs = (source * depth + tile * TILE + row).reshape(-1)
    outputs = np.concatenate([inputs[: 2 * GROUP * TILE], inputs[2 * GROUP * TILE :].reshape(GROUP, TILE).T.reshape(-1)])
    eye = np.eye(width, dtype=jnp.bfloat16)
    return eye[:, inputs], eye[outputs]


def spread_kernel(ancestors, states, w_in, w_out, out_ref, local):
    y, c = lax.axis_index("y"), lax.axis_index("c")
    part_count, rows, width = states.shape
    half = width // 2
    both = 2 * PIECE
    out_row, in_row = iotas((part_count * rows, part_count * rows))
    group, part, row = out_row // both, out_row // PIECE % 2, out_row % PIECE
    onehot = in_row == part * rows + group * PIECE + row
    moved = reorder(onehot, states[...].reshape(part_count * rows, width))
    for h in range(2):
        out_ref[:, h, :, :half] = (
            moved[:, h * half : (h + 1) * half].reshape(-1, both, half).astype(jnp.bfloat16)
        )
    depth = w_out.shape[0]
    mine = pl.ds(pl.multiple_of(c * width, 128), width)
    local[: 2 * depth] = w_in[:, :, mine].astype(jnp.float32).reshape(2 * depth, width)
    local[2 * depth :] = w_out[:, mine].astype(jnp.float32)
    lanes = pl.ds(pl.multiple_of(lax.rem(y, 2) * half, 128), half)
    tile_row = lax.broadcasted_iota(jnp.int32, (both, 128), 0)
    names = jnp.where(tile_row == 3, ancestors[0], ancestors[1]).astype(jnp.float32)
    groups = GROUP // NX // 2
    for x in range(NX):
        e = 2 * x + y // 2
        tile = local[pl.ds(pl.multiple_of(e * TILE, TILE), TILE), lanes]
        extra = local[pl.ds(TILES * TILE + e, 1), lanes]
        last = names
        for i in range(3):
            last = jnp.where(tile_row == i, extra[:, i * 128 : (i + 1) * 128], last)
        at = slice(x * groups, (x + 1) * groups)
        shape = (groups, 2, both)
        out_ref[at, :, :, half:width] = jnp.broadcast_to(tile.astype(jnp.bfloat16), shape + (half,))
        out_ref[at, :, :, width:] = jnp.broadcast_to(last.astype(jnp.bfloat16), shape + (128,))


def pick_kernel(pieces, picked_ref, weights_ref):
    c = lax.axis_index("c")
    half = picked_ref.shape[2]
    width = 2 * half
    rows = pieces[...].astype(jnp.float32).reshape(-1, width + 128)
    count = rows.shape[0]
    last = rows[:, width:].astype(jnp.bfloat16)
    out_row, in_row = iotas((count, count))
    part = lax.rem(out_row // PIECE + c, 2)
    names = reorder(in_row == out_row // TILE * TILE + 3 + part, last)[:, :1]
    onehot = in_row == names.astype(jnp.int32) * PIECE + out_row % PIECE
    picked = reorder(onehot, rows[:, :half].astype(jnp.bfloat16))
    picked_ref[...] = picked.reshape(picked_ref.shape).astype(jnp.bfloat16)
    weights_ref[:count] = rows[:, half:width].astype(jnp.bfloat16)
    out_row, in_row = iotas((GROUP, count))
    for i in range(3):
        extra = reorder(in_row == out_row * TILE + i, last).astype(jnp.bfloat16)
        weights_ref[count:, i * 128 : (i + 1) * 128] = extra


def column_kernel(w0, w1, w2, w3, out_ref):
    half = w0.shape[1]
    for k, block in enumerate((w0, w1, w2, w3)):
        y = lax.rem(lax.axis_index("y") + (NY - k), NY)
        lanes = pl.ds(pl.multiple_of(lax.rem(y, 2) * half, 128), half)
        out_ref[y // 2, :, lanes] = block[...]


def assemble(pieces, part, width):
    both = 2 * PIECE
    half = width // 2
    count = pieces.shape[0] // 2 * both
    out_row, in_row = iotas((count // 2, count))
    onehot = in_row == out_row // PIECE * both + part * PIECE + out_row % PIECE
    sides = []
    for h in range(2):
        values = pieces[:, :, :].reshape(-1, 2, both, half)[:, h]
        values = values.astype(jnp.float32).reshape(count, half).astype(jnp.bfloat16)
        sides.append(reorder(onehot, values))
    return jnp.concatenate(sides, axis=1)


def chip_rows(mine, theirs, width):
    return jnp.concatenate([assemble(mine, 0, width), assemble(theirs, 1, width)], axis=0)


def store_rows(ref, values):
    c = lax.axis_index("c")
    half = values.shape[0] // 2
    for slot, at in ((c, 0), (1 - c, half)):
        ref[pl.ds(pl.multiple_of(slot * half, half), half), :] = values[at : at + half].astype(ref.dtype)


def own_kernel(mine, theirs, gain, _bias, x_ref, normed_ref):
    rows = chip_rows(mine, theirs, x_ref.shape[1])
    x_ref[...] = rows.astype(jnp.bfloat16)
    store_rows(normed_ref, rms_norm(rows, gain[...][None, :]))


def project_kernel(normed, w_qkv, queries_ref, keys_ref, values_ref):
    width = keys_ref.shape[1]
    projected = jnp.dot(normed[...], w_qkv[...], preferred_element_type=jnp.float32)
    scale = 1.0 / math.sqrt(width // HEADS)
    store_rows(queries_ref, projected[:, :width] * scale)
    keys_ref[...] = projected[:, width : 2 * width].astype(jnp.bfloat16)
    values_ref[...] = projected[:, 2 * width :].astype(jnp.bfloat16)


def other_kernel(normed, w_qkv, *refs):
    keys_ref, values_ref = refs[-2:]
    width = keys_ref.shape[1]
    projected = jnp.dot(normed[...], w_qkv[:, width:], preferred_element_type=jnp.float32)
    keys_ref[...] = projected[:, :width].astype(jnp.bfloat16)
    values_ref[...] = projected[:, width:].astype(jnp.bfloat16)


def halves_kernel(left, right, _after, left_ref, right_ref, sent):
    copies = [
        pltpu.make_async_copy(left.at[:1], left_ref, sent.at[0]),
        pltpu.make_async_copy(right.at[1:], right_ref, sent.at[1]),
    ]
    for copy in copies:
        copy.start()
    for copy in copies:
        copy.wait()


def attention_kernel(
    k0, k1, k2, k3, v0, v1, v2, v3, queries, x_rows, bias_own, bias_other, mask, w_o, gain_ff, order,
    _left, _right, stream_ref, normed_ff_ref, keys, values, attended, bias, w_o_here, order_here, loaded,
):
    y = lax.axis_index("y")
    row_count, width = queries.shape
    half = row_count // 2
    head_size = width // HEADS
    together = 4
    loads = []
    for i in range(HEADS // together):
        part = pl.ds(i * together, together)
        for j, source in enumerate((bias_own, bias_other)):
            at = pl.ds(j * half, half)
            loads.append(
                pltpu.make_async_copy(source.at[part], bias.at[part, at], loaded.at[2 * i + j])
            )
    later = [
        pltpu.make_async_copy(w_o, w_o_here, loaded.at[len(loads)]),
        pltpu.make_async_copy(order, order_here, loaded.at[len(loads) + 1]),
    ]
    for copy in loads + later:
        copy.start()
    for k, (key_block, value_block) in enumerate(((k0, v0), (k1, v1), (k2, v2), (k3, v3))):
        at = pl.multiple_of(lax.rem(y + (NY - k), NY) * row_count, row_count)
        keys[pl.ds(at, row_count), :] = key_block[...]
        values[pl.ds(at, row_count), :] = value_block[...]
    unusable = jnp.where(mask[...][None, :] > 0, 0.0, -1e30)
    attended[...] = jnp.zeros_like(attended)
    for start in range(0, HEADS, together):
        heads = []
        for h in range(start, start + together):
            first, last = h * head_size, (h + 1) * head_size
            lo, hi = first // 128 * 128, -(-last // 128) * 128
            lanes = lax.broadcasted_iota(jnp.int32, (1, hi - lo), 1) + lo
            heads.append((h, lo, hi, (lanes >= first) & (lanes < last)))
        scores = [
            lax.dot_general(
                jnp.where(inside, queries[:, lo:hi], jnp.zeros((), jnp.bfloat16)),
                keys[:, lo:hi],
                (((1,), (1,)), ((), ())),
                preferred_element_type=jnp.float32,
            )
            for _, lo, hi, inside in heads
        ]
        for j in range(2):
            loads[2 * (start // together) + j].wait()
        weights, totals = [], []
        for (h, _, _, _), score in zip(heads, scores):
            score = score + bias[h].astype(jnp.float32) + unusable
            weight = jnp.exp(score - jnp.max(score, axis=1, keepdims=True))
            totals.append(jnp.sum(weight, axis=1, keepdims=True))
            weights.append(weight.astype(jnp.bfloat16))
        for (_, lo, hi, inside), weight, total in zip(heads, weights, totals):
            mixture = jnp.dot(weight, values[:, lo:hi], preferred_element_type=jnp.float32)
            attended[:, lo:hi] += jnp.where(inside, mixture / total, 0.0)
    for copy in later:
        copy.wait()
    stream = x_rows[...].astype(jnp.float32) + jnp.dot(
        attended[...].astype(jnp.bfloat16), w_o_here[...], preferred_element_type=jnp.float32
    )
    stream_ref[...] = stream
    normed_ff = rms_norm(stream, gain_ff[...][None, :]).astype(jnp.bfloat16)
    normed_ff_ref[...] = jnp.dot(
        normed_ff, order_here[...], preferred_element_type=jnp.float32
    ).astype(jnp.bfloat16)


def transition_kernel(
    own, other, stream, order, here, left, right, far_0, far_1, keep_ref, send_ref,
    tiles, extras, arrived,
):
    c, x = lax.axis_index("c"), lax.axis_index("x")
    half = own.shape[0] // 2
    width = own.shape[1]
    count = tiles.shape[1]
    far = lax.rem(x + 2, NX) * 2
    parts = [
        (here, pl.ds(x * 2, 2)),
        (left, pl.ds(lax.rem(x + 3, NX) * 2, 2)),
        (right, pl.ds(lax.rem(x + 1, NX) * 2, 2)),
        (far_0, pl.ds(far, 1)),
        (far_1, pl.ds(far + 1, 1)),
    ]
    copies = []
    for k, (block, at) in enumerate(parts):
        copies.append(pltpu.make_async_copy(block.at[:, :count], tiles.at[at], arrived.at[2 * k]))
        copies.append(pltpu.make_async_copy(block.at[:, count:], extras.at[at], arrived.at[2 * k + 1]))
    for copy in copies:
        copy.start()
    rows = jnp.concatenate([own[...], other[...]], axis=0)
    for copy in copies:
        copy.wait()
    gate = jnp.dot(rows, tiles[0:3].reshape(width, width), preferred_element_type=jnp.float32)
    up = jnp.dot(rows, tiles[3:6].reshape(width, width), preferred_element_type=jnp.float32)
    hidden = (gate / (1.0 + jnp.exp(-gate)) * up).astype(jnp.bfloat16)
    across = (((1,), (1,)), ((), ()))
    update = jnp.concatenate(
        [
            lax.dot_general(
                hidden, tiles[6:8].reshape(2 * count, width), across, preferred_element_type=jnp.float32
            ),
            lax.dot_general(
                hidden, extras[...].reshape(-1, width), across, preferred_element_type=jnp.float32
            ),
        ],
        axis=1,
    )
    high = update.astype(jnp.bfloat16)
    low = (update - high.astype(jnp.float32)).astype(jnp.bfloat16)
    update = jnp.dot(high, order[...], preferred_element_type=jnp.float32) + jnp.dot(
        low, order[...], preferred_element_type=jnp.float32
    )
    keep_ref[c] = update[:half] + stream[:half]
    send_ref[c] = update[half : 2 * half] + stream[half:]
    send_ref[1 - c] = update[2 * half : 3 * half]
    keep_ref[1 - c] = update[3 * half :]


def swap_cores(value):
    return lax.ppermute(value, "c", [(0, 1), (1, 0)])


def others(value, axis, size):
    return [
        lax.ppermute(value, axis, [(i, (i + k) % size) for i in range(size)]) for k in range(1, size)
    ]


def kernel(f, name, specs, args, shapes, limit=8, scratch=(), out_spec=None, wait=1):
    def whole(shape):
        return pl.BlockSpec(shape, lambda i: (0,) * len(shape))

    specs = [whole(a.shape) if s is None else s for s, a in zip(specs, args, strict=True)]
    outs = tuple(jax.ShapeDtypeStruct(shape, dtype) for shape, dtype in shapes)
    return pl.pallas_call(
        f,
        grid=(1,),
        out_shape=outs,
        in_specs=specs,
        out_specs=tuple(out_spec or whole(o.shape) for o in outs),
        scratch_shapes=scratch,
        compiler_params=pltpu.CompilerParams(vmem_limit_bytes=limit * MIB),
        cost_estimate=pl.CostEstimate(
            flops=int(wait * MICROSECOND), bytes_accessed=0, transcendentals=0
        ),
        name=name,
    )(*args)


def body(states, ancestors, pair_bias, key_mask, gain_attn, w_qkv, w_o, gain_ff, w_in, w_out):
    part_count, block_rows, width = states.shape
    rows = block_rows * NC
    half = width // 2
    both = 2 * PIECE
    depth = w_out.shape[0]
    bf16, f32 = jnp.bfloat16, jnp.float32
    order_in, order_out = weight_orders(width)

    bias_other = swap_cores(pair_bias)
    (pieces,) = kernel(
        spread_kernel,
        "spread",
        [SMEM, None, None, None],
        (ancestors, states, w_in, w_out),
        [((GROUP // 2, 2, both, width + 128), bf16)],
        limit=56,
        scratch=[pltpu.VMEM((3 * depth, width), f32)],
    )
    pieces = lax.all_to_all(pieces.reshape(GROUP, both, width + 128), PARTICLE, 0, 0)
    picked, piece = kernel(
        pick_kernel,
        "pick",
        [None],
        (pieces,),
        [((GROUP, both, half), bf16), ((GROUP * (TILE + 1), half), bf16)],
        limit=40,
    )
    ring = [piece] + others(piece, "y", NY)
    (column,) = kernel(
        column_kernel,
        "column",
        [None] * NY,
        ring,
        [((2, GROUP * (TILE + 1), width), bf16)],
    )
    forward, back = ([(i, (i + k) % NX) for i in range(NX)] for k in (1, -1))
    left, right = lax.ppermute(column, "x", forward), lax.ppermute(column, "x", back)

    mine = lax.all_to_all(picked, PARTICLE, 0, 0)
    x_rows, normed = kernel(
        own_kernel,
        "own",
        [None, None, None, ANY],
        (mine, swap_cores(mine), gain_attn, bias_other),
        [((rows, width), bf16)] * 2,
    )
    queries, *own = kernel(
        project_kernel, "project", [None, VMEM], (normed, w_qkv), [((rows, width), bf16)] * 3
    )
    blocks = others(normed, "y", NY)
    made = [
        kernel(other_kernel, "other", [None, VMEM], (block, w_qkv), [((rows, width), bf16)] * 2)
        for block in blocks[1:]
    ]
    left_half, right_half = kernel(
        halves_kernel,
        "halves",
        [ANY] * 3,
        (left, right, made[0][0]),
        [((1,) + column.shape[1:], bf16)] * 2,
        out_spec=ANY,
        scratch=[pltpu.SemaphoreType.DMA((2,))],
    )
    first = kernel(
        other_kernel,
        "other",
        [None, VMEM, ANY, ANY],
        (blocks[0], w_qkv, left_half, right_half),
        [((rows, width), bf16)] * 2,
    )
    made = [own, first] + made
    far = [lax.ppermute(left_half, "x", forward), lax.ppermute(right_half, "x", back)]
    stream, normed_ff = kernel(
        attention_kernel,
        "attention",
        [None] * 10 + [ANY, ANY, None, ANY, None] + [ANY] * 3,
        (
            *[k for k, _ in made], *[v for _, v in made], queries, x_rows, pair_bias, bias_other,
            key_mask, w_o, gain_ff, order_in, left_half, right_half,
        ),
        [((rows, width), f32), ((rows, width), bf16)],
        limit=16,
        wait=4,
        scratch=[
            pltpu.VMEM((rows * NY, width), bf16),
            pltpu.VMEM((rows * NY, width), bf16),
            pltpu.VMEM((rows, width), f32),
            pltpu.VMEM((HEADS, rows, rows * NY), bf16),
            pltpu.VMEM((width, width), bf16),
            pltpu.VMEM((width, width), bf16),
            pltpu.SemaphoreType.DMA((10,)),
        ],
    )
    keep, send = kernel(
        transition_kernel,
        "transition",
        [None] * 4 + [ANY] * 5,
        (normed_ff, swap_cores(normed_ff), stream, order_out, column, left, right, *far),
        [((part_count, block_rows, width), f32)] * 2,
        limit=16,
        scratch=[
            pltpu.VMEM((TILES, GROUP * TILE, width), bf16),
            pltpu.VMEM((TILES, GROUP, width), bf16),
            pltpu.SemaphoreType.DMA((10,)),
        ],
    )
    return (keep + swap_cores(send)).astype(bf16)


def solution(mesh):
    fine = Mesh(mesh.devices.reshape(NX, NZ, NY, NC), ("x", "z", "y", "c"))
    token = ("y", "c")
    placed = (
        P(PARTICLE, token, None),
        P(PARTICLE),
        P(None, token, None),
        P(),
        P(),
        P(),
        P(),
        P(),
        P(None, PARTICLE, None),
        P(PARTICLE, None),
    )
    return jax.shard_map(
        body, mesh=fine, in_specs=placed, out_specs=P(PARTICLE, token, None), check_vma=False
    )
```

```python
import math

import jax
import jax.numpy as jnp
import numpy as np
from jax import lax
from jax.experimental import pallas as pl
from jax.experimental.pallas import tpu as pltpu
from jax.sharding import Mesh
from jax.sharding import PartitionSpec as P

NX, NZ, NY, NC = 4, 8, 4, 2
GROUP = NX * NZ
PARTICLE = ("x", "z")
HEADS = 16
EPS = 1e-05
PIECE = 4
TILE = 8
TILES = 8
MIB = 2**20
MICROSECOND = 10**9
ANY = pl.BlockSpec(memory_space=pl.ANY)
VMEM = pl.BlockSpec(memory_space=pltpu.VMEM)
SMEM = pl.BlockSpec(memory_space=pltpu.SMEM)


def rms_norm(stream, gain_vec):
    return stream * lax.rsqrt(jnp.mean(stream * stream, axis=-1, keepdims=True) + EPS) * gain_vec


def iotas(shape):
    return lax.broadcasted_iota(jnp.int32, shape, 0), lax.broadcasted_iota(jnp.int32, shape, 1)


def reorder(onehot, values):
    return jnp.dot(onehot.astype(jnp.bfloat16), values, preferred_element_type=jnp.float32)


def input_order(width):
    depth = width // GROUP
    tile, source, row = np.meshgrid(np.arange(3), np.arange(GROUP), np.arange(TILE), indexing="ij")
    return np.eye(width, dtype=jnp.bfloat16)[:, (source * depth + tile * TILE + row).reshape(-1)]


def spread_kernel(ancestors, states, w_in, w_out, out_ref, local):
    y, c = lax.axis_index("y"), lax.axis_index("c")
    part_count, rows, width = states.shape
    half = width // 2
    both = 2 * PIECE
    out_row, in_row = iotas((part_count * rows, part_count * rows))
    group, part, row = out_row // both, out_row // PIECE % 2, out_row % PIECE
    onehot = in_row == part * rows + group * PIECE + row
    moved = reorder(onehot, states[...].reshape(part_count * rows, width))
    for h in range(2):
        out_ref[:, h, :, :half] = (
            moved[:, h * half : (h + 1) * half].reshape(-1, both, half).astype(jnp.bfloat16)
        )
    depth = w_out.shape[0]
    mine = pl.ds(pl.multiple_of(c * width, 128), width)
    local[: 2 * depth] = w_in[:, :, mine].astype(jnp.float32).reshape(2 * depth, width)
    local[2 * depth :] = w_out[:, mine].astype(jnp.float32)
    lanes = pl.ds(pl.multiple_of(lax.rem(y, 2) * half, 128), half)
    tile_row = lax.broadcasted_iota(jnp.int32, (both, 128), 0)
    names = jnp.where(tile_row == 3, ancestors[0], ancestors[1]).astype(jnp.float32)
    groups = GROUP // NX // 2
    for x in range(NX):
        e = 2 * x + y // 2
        tile = local[pl.ds(pl.multiple_of(e * TILE, TILE), TILE), lanes]
        extra = local[pl.ds(TILES * TILE + e, 1), lanes]
        last = names
        for i in range(3):
            last = jnp.where(tile_row == i, extra[:, i * 128 : (i + 1) * 128], last)
        at = slice(x * groups, (x + 1) * groups)
        shape = (groups, 2, both)
        out_ref[at, :, :, half:width] = jnp.broadcast_to(tile.astype(jnp.bfloat16), shape + (half,))
        out_ref[at, :, :, width:] = jnp.broadcast_to(last.astype(jnp.bfloat16), shape + (128,))


def pick_kernel(pieces, picked_ref, weights_ref):
    c = lax.axis_index("c")
    half = picked_ref.shape[2]
    width = 2 * half
    rows = pieces[...].astype(jnp.float32).reshape(-1, width + 128)
    count = rows.shape[0]
    last = rows[:, width:].astype(jnp.bfloat16)
    out_row, in_row = iotas((count, count))
    part = lax.rem(out_row // PIECE + c, 2)
    names = reorder(in_row == out_row // TILE * TILE + 3 + part, last)[:, :1]
    onehot = in_row == names.astype(jnp.int32) * PIECE + out_row % PIECE
    picked = reorder(onehot, rows[:, :half].astype(jnp.bfloat16))
    picked_ref[...] = picked.reshape(picked_ref.shape).astype(jnp.bfloat16)
    weights_ref[:count] = rows[:, half:width].astype(jnp.bfloat16)
    out_row, in_row = iotas((GROUP, count))
    for i in range(3):
        extra = reorder(in_row == out_row * TILE + i, last).astype(jnp.bfloat16)
        weights_ref[count:, i * 128 : (i + 1) * 128] = extra


def column_kernel(w0, w1, w2, w3, out_ref):
    half = w0.shape[1]
    for k, block in enumerate((w0, w1, w2, w3)):
        y = lax.rem(lax.axis_index("y") + (NY - k), NY)
        lanes = pl.ds(pl.multiple_of(lax.rem(y, 2) * half, 128), half)
        out_ref[y // 2, :, lanes] = block[...]


def assemble(pieces, part, width):
    both = 2 * PIECE
    half = width // 2
    count = pieces.shape[0] // 2 * both
    out_row, in_row = iotas((count // 2, count))
    onehot = in_row == out_row // PIECE * both + part * PIECE + out_row % PIECE
    sides = []
    for h in range(2):
        values = pieces[:, :, :].reshape(-1, 2, both, half)[:, h]
        values = values.astype(jnp.float32).reshape(count, half).astype(jnp.bfloat16)
        sides.append(reorder(onehot, values))
    return jnp.concatenate(sides, axis=1)


def chip_rows(mine, theirs, width):
    return jnp.concatenate([assemble(mine, 0, width), assemble(theirs, 1, width)], axis=0)


def store_rows(ref, values):
    c = lax.axis_index("c")
    half = values.shape[0] // 2
    for slot, at in ((c, 0), (1 - c, half)):
        ref[pl.ds(pl.multiple_of(slot * half, half), half), :] = values[at : at + half].astype(ref.dtype)


def own_kernel(mine, theirs, gain, _bias, x_ref, normed_ref):
    rows = chip_rows(mine, theirs, x_ref.shape[1])
    x_ref[...] = rows.astype(jnp.bfloat16)
    store_rows(normed_ref, rms_norm(rows, gain[...][None, :]))


def project_kernel(normed, w_qkv, queries_ref, keys_ref, values_ref):
    width = keys_ref.shape[1]
    projected = jnp.dot(normed[...], w_qkv[...], preferred_element_type=jnp.float32)
    scale = 1.0 / math.sqrt(width // HEADS)
    store_rows(queries_ref, projected[:, :width] * scale)
    keys_ref[...] = projected[:, width : 2 * width].astype(jnp.bfloat16)
    values_ref[...] = projected[:, 2 * width :].astype(jnp.bfloat16)


def other_kernel(normed, w_qkv, *refs):
    keys_ref, values_ref = refs[-2:]
    width = keys_ref.shape[1]
    projected = jnp.dot(normed[...], w_qkv[:, width:], preferred_element_type=jnp.float32)
    keys_ref[...] = projected[:, :width].astype(jnp.bfloat16)
    values_ref[...] = projected[:, width:].astype(jnp.bfloat16)


def halves_kernel(left, right, _after, left_ref, right_ref, sent):
    copies = [
        pltpu.make_async_copy(left.at[:1], left_ref, sent.at[0]),
        pltpu.make_async_copy(right.at[1:], right_ref, sent.at[1]),
    ]
    for copy in copies:
        copy.start()
    for copy in copies:
        copy.wait()


def attention_kernel(
    k0, k1, k2, k3, v0, v1, v2, v3, queries, x_rows, bias_own, bias_other, mask, w_o, gain_ff, order,
    _left, _right, stream_ref, normed_ff_ref, keys, values, attended, bias, w_o_here, order_here, loaded,
):
    y = lax.axis_index("y")
    row_count, width = queries.shape
    half = row_count // 2
    head_size = width // HEADS
    together = 8
    loads = []
    for i in range(HEADS // together):
        part = pl.ds(i * together, together)
        for j, source in enumerate((bias_own, bias_other)):
            at = pl.ds(j * half, half)
            loads.append(
                pltpu.make_async_copy(source.at[part], bias.at[part, at], loaded.at[2 * i + j])
            )
    later = [
        pltpu.make_async_copy(w_o, w_o_here, loaded.at[len(loads)]),
        pltpu.make_async_copy(order, order_here, loaded.at[len(loads) + 1]),
    ]
    for copy in loads + later:
        copy.start()
    for k, (key_block, value_block) in enumerate(((k0, v0), (k1, v1), (k2, v2), (k3, v3))):
        at = pl.multiple_of(lax.rem(y + (NY - k), NY) * row_count, row_count)
        keys[pl.ds(at, row_count), :] = key_block[...]
        values[pl.ds(at, row_count), :] = value_block[...]
    unusable = jnp.where(mask[...][None, :] > 0, 0.0, -1e30)
    attended[...] = jnp.zeros_like(attended)
    for start in range(0, HEADS, together):
        heads = []
        for h in range(start, start + together):
            first, last = h * head_size, (h + 1) * head_size
            lo, hi = first // 128 * 128, -(-last // 128) * 128
            lanes = lax.broadcasted_iota(jnp.int32, (1, hi - lo), 1) + lo
            heads.append((h, lo, hi, (lanes >= first) & (lanes < last)))
        scores = [
            lax.dot_general(
                jnp.where(inside, queries[:, lo:hi], jnp.zeros((), jnp.bfloat16)),
                keys[:, lo:hi],
                (((1,), (1,)), ((), ())),
                preferred_element_type=jnp.float32,
            )
            for _, lo, hi, inside in heads
        ]
        for j in range(2):
            loads[2 * (start // together) + j].wait()
        weights, totals = [], []
        for (h, _, _, _), score in zip(heads, scores):
            score = score + bias[h].astype(jnp.float32) + unusable
            weight = jnp.exp(score - jnp.max(score, axis=1, keepdims=True))
            totals.append(jnp.sum(weight, axis=1, keepdims=True))
            weights.append(weight.astype(jnp.bfloat16))
        for (_, lo, hi, inside), weight, total in zip(heads, weights, totals):
            mixture = jnp.dot(weight, values[:, lo:hi], preferred_element_type=jnp.float32)
            attended[:, lo:hi] += jnp.where(inside, mixture / total, 0.0)
    for copy in later:
        copy.wait()
    stream = x_rows[...].astype(jnp.float32) + jnp.dot(
        attended[...].astype(jnp.bfloat16), w_o_here[...], preferred_element_type=jnp.float32
    )
    stream_ref[...] = stream
    normed_ff = rms_norm(stream, gain_ff[...][None, :]).astype(jnp.bfloat16)
    normed_ff_ref[...] = jnp.dot(
        normed_ff, order_here[...], preferred_element_type=jnp.float32
    ).astype(jnp.bfloat16)


def transition_kernel(
    own, other, stream, here, left, right, far_0, far_1, keep_ref, send_ref, weights, extras, arrived
):
    c, x = lax.axis_index("c"), lax.axis_index("x")
    half = own.shape[0] // 2
    width = own.shape[1]
    parts = [(block.at[i], across, i) for block, across in ((here, 0), (left, 3), (right, 1)) for i in range(2)]
    parts += [(far_0.at[0], 2, 0), (far_1.at[0], 2, 1)]
    copies = []
    for k, (part, across, i) in enumerate(parts):
        e = lax.rem(x + across, NX) * 2 + i
        copies.append(pltpu.make_async_copy(part.at[:GROUP], weights.at[e], arrived.at[2 * k]))
        copies.append(pltpu.make_async_copy(part.at[GROUP:], extras.at[e], arrived.at[2 * k + 1]))
    for copy in copies:
        copy.start()
    rows = jnp.concatenate([own[...], other[...]], axis=0)
    for copy in copies:
        copy.wait()

    def plain(tiles):
        return tiles.astype(jnp.float32).reshape(-1, width).astype(jnp.bfloat16)

    gate = jnp.dot(rows, weights[0:3].reshape(width, width), preferred_element_type=jnp.float32)
    up = jnp.dot(rows, weights[3:6].reshape(width, width), preferred_element_type=jnp.float32)
    out_row, in_row = iotas((GROUP * TILE, GROUP * TILE))
    onehot = in_row == out_row % TILE * GROUP + out_row // TILE
    last = reorder(onehot, plain(extras[...])).reshape(GROUP, 1, TILE, width)
    first = [weights[e].astype(jnp.float32).reshape(GROUP, 1, TILE, width) for e in (6, 7)]
    down = jnp.concatenate([*first, last], axis=1).reshape(width, width).astype(jnp.bfloat16)
    hidden = (gate / (1.0 + jnp.exp(-gate)) * up).astype(jnp.bfloat16)
    update = lax.dot_general(
        hidden, down, (((1,), (1,)), ((), ())), preferred_element_type=jnp.float32
    )
    keep_ref[c] = update[:half] + stream[:half]
    send_ref[c] = (update[half : 2 * half] + stream[half:]).astype(jnp.bfloat16)
    send_ref[1 - c] = update[2 * half : 3 * half].astype(jnp.bfloat16)
    keep_ref[1 - c] = update[3 * half :]


def swap_cores(value):
    return lax.ppermute(value, "c", [(0, 1), (1, 0)])


def others(value, axis, size):
    return [
        lax.ppermute(value, axis, [(i, (i + k) % size) for i in range(size)]) for k in range(1, size)
    ]


def kernel(f, name, specs, args, shapes, limit=8, scratch=(), out_spec=None, wait=1):
    def whole(shape):
        return pl.BlockSpec(shape, lambda i: (0,) * len(shape))

    specs = [whole(a.shape) if s is None else s for s, a in zip(specs, args, strict=True)]
    outs = tuple(jax.ShapeDtypeStruct(shape, dtype) for shape, dtype in shapes)
    return pl.pallas_call(
        f,
        grid=(1,),
        out_shape=outs,
        in_specs=specs,
        out_specs=tuple(out_spec or whole(o.shape) for o in outs),
        scratch_shapes=scratch,
        compiler_params=pltpu.CompilerParams(vmem_limit_bytes=limit * MIB),
        cost_estimate=pl.CostEstimate(
            flops=int(wait * MICROSECOND), bytes_accessed=0, transcendentals=0
        ),
        name=name,
    )(*args)


def body(states, ancestors, pair_bias, key_mask, gain_attn, w_qkv, w_o, gain_ff, w_in, w_out):
    part_count, block_rows, width = states.shape
    rows = block_rows * NC
    half = width // 2
    both = 2 * PIECE
    depth = w_out.shape[0]
    bf16, f32 = jnp.bfloat16, jnp.float32
    order_in = input_order(width)

    bias_other = swap_cores(pair_bias)
    (pieces,) = kernel(
        spread_kernel,
        "spread",
        [SMEM, None, None, None],
        (ancestors, states, w_in, w_out),
        [((GROUP // 2, 2, both, width + 128), bf16)],
        limit=56,
        scratch=[pltpu.VMEM((3 * depth, width), f32)],
    )
    pieces = lax.all_to_all(pieces.reshape(GROUP, both, width + 128), PARTICLE, 0, 0)
    picked, piece = kernel(
        pick_kernel,
        "pick",
        [None],
        (pieces,),
        [((GROUP, both, half), bf16), ((GROUP * (TILE + 1), half), bf16)],
        limit=40,
    )
    ring = [piece] + others(piece, "y", NY)
    (column,) = kernel(
        column_kernel,
        "column",
        [None] * NY,
        ring,
        [((2, GROUP * (TILE + 1), width), bf16)],
    )
    forward, back = ([(i, (i + k) % NX) for i in range(NX)] for k in (1, -1))
    left, right = lax.ppermute(column, "x", forward), lax.ppermute(column, "x", back)

    mine = lax.all_to_all(picked, PARTICLE, 0, 0)
    x_rows, normed = kernel(
        own_kernel,
        "own",
        [None, None, None, ANY],
        (mine, swap_cores(mine), gain_attn, bias_other),
        [((rows, width), bf16)] * 2,
    )
    queries, *own = kernel(
        project_kernel, "project", [None, VMEM], (normed, w_qkv), [((rows, width), bf16)] * 3
    )
    blocks = others(normed, "y", NY)
    made = [
        kernel(other_kernel, "other", [None, VMEM], (block, w_qkv), [((rows, width), bf16)] * 2)
        for block in blocks[1:]
    ]
    left_half, right_half = kernel(
        halves_kernel,
        "halves",
        [ANY] * 3,
        (left, right, made[0][0]),
        [((1,) + column.shape[1:], bf16)] * 2,
        out_spec=ANY,
        scratch=[pltpu.SemaphoreType.DMA((2,))],
    )
    first = kernel(
        other_kernel,
        "other",
        [None, VMEM, ANY, ANY],
        (blocks[0], w_qkv, left_half, right_half),
        [((rows, width), bf16)] * 2,
    )
    made = [own, first] + made
    far = [lax.ppermute(left_half, "x", forward), lax.ppermute(right_half, "x", back)]
    stream, normed_ff = kernel(
        attention_kernel,
        "attention",
        [None] * 10 + [ANY, ANY, None, ANY, None] + [ANY] * 3,
        (
            *[k for k, _ in made], *[v for _, v in made], queries, x_rows, pair_bias, bias_other,
            key_mask, w_o, gain_ff, order_in, left_half, right_half,
        ),
        [((rows, width), f32), ((rows, width), bf16)],
        limit=16,
        wait=4,
        scratch=[
            pltpu.VMEM((rows * NY, width), bf16),
            pltpu.VMEM((rows * NY, width), bf16),
            pltpu.VMEM((rows, width), f32),
            pltpu.VMEM((HEADS, rows, rows * NY), bf16),
            pltpu.VMEM((width, width), bf16),
            pltpu.VMEM((width, width), bf16),
            pltpu.SemaphoreType.DMA((6,)),
        ],
    )
    keep, send = kernel(
        transition_kernel,
        "transition",
        [None] * 3 + [ANY] * 5,
        (
            normed_ff, swap_cores(normed_ff), stream,
            *(w.reshape(w.shape[0], -1, TILE, width) for w in (column, left, right, *far)),
        ),
        [((part_count, block_rows, width), t) for t in (f32, bf16)],
        limit=16,
        scratch=[
            pltpu.VMEM((TILES, GROUP, TILE, width), bf16),
            pltpu.VMEM((TILES, GROUP // TILE, TILE, width), bf16),
            pltpu.SemaphoreType.DMA((16,)),
        ],
    )
    return (keep + swap_cores(send)).astype(bf16)


def solution(mesh):
    fine = Mesh(mesh.devices.reshape(NX, NZ, NY, NC), ("x", "z", "y", "c"))
    token = ("y", "c")
    placed = (
        P(PARTICLE, token, None),
        P(PARTICLE),
        P(None, token, None),
        P(),
        P(),
        P(),
        P(),
        P(),
        P(None, PARTICLE, None),
        P(PARTICLE, None),
    )
    return jax.shard_map(
        body, mesh=fine, in_specs=placed, out_specs=P(PARTICLE, token, None), check_vma=False
    )
```

```python
import math

import jax
import jax.numpy as jnp
import numpy as np
from jax import lax
from jax.experimental import pallas as pl
from jax.experimental.pallas import tpu as pltpu
from jax.sharding import Mesh
from jax.sharding import PartitionSpec as P

NX, NZ, NY, NC = 4, 8, 4, 2
GROUP = NX * NZ
PARTICLE = ("x", "z")
HEADS = 16
EPS = 1e-05
PIECE = 4
TILE = 8
TILES = 8
MIB = 2**20
MICROSECOND = 10**9
ANY = pl.BlockSpec(memory_space=pl.ANY)
VMEM = pl.BlockSpec(memory_space=pltpu.VMEM)
SMEM = pl.BlockSpec(memory_space=pltpu.SMEM)


def rms_norm(stream, gain_vec):
    return stream * lax.rsqrt(jnp.mean(stream * stream, axis=-1, keepdims=True) + EPS) * gain_vec


def iotas(shape):
    return lax.broadcasted_iota(jnp.int32, shape, 0), lax.broadcasted_iota(jnp.int32, shape, 1)


def reorder(onehot, values):
    return jnp.dot(onehot.astype(jnp.bfloat16), values, preferred_element_type=jnp.float32)


def input_order(width):
    depth = width // GROUP
    tile, source, row = np.meshgrid(np.arange(3), np.arange(GROUP), np.arange(TILE), indexing="ij")
    return np.eye(width, dtype=jnp.bfloat16)[:, (source * depth + tile * TILE + row).reshape(-1)]


def spread_kernel(ancestors, states, w_in, w_out, out_ref, local):
    y, c = lax.axis_index("y"), lax.axis_index("c")
    part_count, rows, width = states.shape
    half = width // 2
    both = 2 * PIECE
    out_row, in_row = iotas((part_count * rows, part_count * rows))
    group, part, row = out_row // both, out_row // PIECE % 2, out_row % PIECE
    onehot = in_row == part * rows + group * PIECE + row
    moved = reorder(onehot, states[...].reshape(part_count * rows, width))
    for h in range(2):
        out_ref[:, h, :, :half] = (
            moved[:, h * half : (h + 1) * half].reshape(-1, both, half).astype(jnp.bfloat16)
        )
    depth = w_out.shape[0]
    mine = pl.ds(pl.multiple_of(c * width, 128), width)
    local[: 2 * depth] = w_in[:, :, mine].astype(jnp.float32).reshape(2 * depth, width)
    local[2 * depth :] = w_out[:, mine].astype(jnp.float32)
    lanes = pl.ds(pl.multiple_of(lax.rem(y, 2) * half, 128), half)
    tile_row = lax.broadcasted_iota(jnp.int32, (both, 128), 0)
    names = jnp.where(tile_row == 3, ancestors[0], ancestors[1]).astype(jnp.float32)
    groups = GROUP // NX // 2
    for x in range(NX):
        e = 2 * x + y // 2
        tile = local[pl.ds(pl.multiple_of(e * TILE, TILE), TILE), lanes]
        extra = local[pl.ds(TILES * TILE + e, 1), lanes]
        last = names
        for i in range(3):
            last = jnp.where(tile_row == i, extra[:, i * 128 : (i + 1) * 128], last)
        at = slice(x * groups, (x + 1) * groups)
        shape = (groups, 2, both)
        out_ref[at, :, :, half:width] = jnp.broadcast_to(tile.astype(jnp.bfloat16), shape + (half,))
        out_ref[at, :, :, width:] = jnp.broadcast_to(last.astype(jnp.bfloat16), shape + (128,))


def unpack_kernel(pieces, states_ref, weights_ref, onehot_ref):
    half = states_ref.shape[1]
    width = 2 * half
    rows = pieces[...].astype(jnp.float32).reshape(-1, width + 128)
    count = rows.shape[0]
    states_ref[...] = rows[:, :half].astype(jnp.bfloat16)
    last = rows[:, width:].astype(jnp.bfloat16)
    weights_ref[:count] = rows[:, half:width].astype(jnp.bfloat16)
    out_row, in_row = iotas((GROUP, count))
    for i in range(3):
        extra = reorder(in_row == out_row * TILE + i, last).astype(jnp.bfloat16)
        weights_ref[count:, i * 128 : (i + 1) * 128] = extra
    out_row, in_row = iotas((count, count))
    part = lax.rem(out_row // PIECE + lax.axis_index("c"), 2)
    names = reorder(in_row == out_row // TILE * TILE + 3 + part, last)[:, :1]
    onehot = in_row == names.astype(jnp.int32) * PIECE + out_row % PIECE
    onehot_ref[...] = onehot.astype(jnp.bfloat16)


def pick_kernel(onehot, states, picked_ref):
    picked = reorder(onehot[...], states[...])
    picked_ref[...] = picked.reshape(picked_ref.shape).astype(jnp.bfloat16)


def column_kernel(w0, w1, w2, w3, out_ref):
    half = w0.shape[1]
    for k, block in enumerate((w0, w1, w2, w3)):
        y = lax.rem(lax.axis_index("y") + (NY - k), NY)
        lanes = pl.ds(pl.multiple_of(lax.rem(y, 2) * half, 128), half)
        out_ref[y // 2, :, lanes] = block[...]


def assemble(pieces, part, width):
    both = 2 * PIECE
    half = width // 2
    count = pieces.shape[0] // 2 * both
    out_row, in_row = iotas((count // 2, count))
    onehot = in_row == out_row // PIECE * both + part * PIECE + out_row % PIECE
    sides = []
    for h in range(2):
        values = pieces[:, :, :].reshape(-1, 2, both, half)[:, h]
        values = values.astype(jnp.float32).reshape(count, half).astype(jnp.bfloat16)
        sides.append(reorder(onehot, values))
    return jnp.concatenate(sides, axis=1)


def chip_rows(mine, theirs, width):
    return jnp.concatenate([assemble(mine, 0, width), assemble(theirs, 1, width)], axis=0)


def store_rows(ref, values):
    c = lax.axis_index("c")
    half = values.shape[0] // 2
    for slot, at in ((c, 0), (1 - c, half)):
        ref[pl.ds(pl.multiple_of(slot * half, half), half), :] = values[at : at + half].astype(ref.dtype)


def own_kernel(mine, theirs, gain, _bias, x_ref, normed_ref):
    rows = chip_rows(mine, theirs, x_ref.shape[1])
    x_ref[...] = rows.astype(jnp.bfloat16)
    store_rows(normed_ref, rms_norm(rows, gain[...][None, :]))


def project_kernel(normed, w_qkv, queries_ref, keys_ref, values_ref):
    width = keys_ref.shape[1]
    projected = jnp.dot(normed[...], w_qkv[...], preferred_element_type=jnp.float32)
    scale = 1.0 / math.sqrt(width // HEADS)
    store_rows(queries_ref, projected[:, :width] * scale)
    keys_ref[...] = projected[:, width : 2 * width].astype(jnp.bfloat16)
    values_ref[...] = projected[:, 2 * width :].astype(jnp.bfloat16)


def other_kernel(normed, w_qkv, *refs):
    keys_ref, values_ref = refs[-2:]
    width = keys_ref.shape[1]
    projected = jnp.dot(normed[...], w_qkv[:, width:], preferred_element_type=jnp.float32)
    keys_ref[...] = projected[:, :width].astype(jnp.bfloat16)
    values_ref[...] = projected[:, width:].astype(jnp.bfloat16)


def halves_kernel(left, right, _after, left_ref, right_ref, sent):
    copies = [
        pltpu.make_async_copy(left.at[:1], left_ref, sent.at[0]),
        pltpu.make_async_copy(right.at[1:], right_ref, sent.at[1]),
    ]
    for copy in copies:
        copy.start()
    for copy in copies:
        copy.wait()


def attention_kernel(
    k0, k1, k2, k3, v0, v1, v2, v3, queries, x_rows, bias_own, bias_other, mask, w_o, gain_ff, order,
    _left, _right, stream_ref, normed_ff_ref, keys, values, attended, bias, w_o_here, order_here, loaded,
):
    y = lax.axis_index("y")
    row_count, width = queries.shape
    half = row_count // 2
    head_size = width // HEADS
    together = 8
    loads = []
    for i in range(HEADS // together):
        part = pl.ds(i * together, together)
        for j, source in enumerate((bias_own, bias_other)):
            at = pl.ds(j * half, half)
            loads.append(
                pltpu.make_async_copy(source.at[part], bias.at[part, at], loaded.at[2 * i + j])
            )
    later = [
        pltpu.make_async_copy(w_o, w_o_here, loaded.at[len(loads)]),
        pltpu.make_async_copy(order, order_here, loaded.at[len(loads) + 1]),
    ]
    for copy in loads + later:
        copy.start()
    for k, (key_block, value_block) in enumerate(((k0, v0), (k1, v1), (k2, v2), (k3, v3))):
        at = pl.multiple_of(lax.rem(y + (NY - k), NY) * row_count, row_count)
        keys[pl.ds(at, row_count), :] = key_block[...]
        values[pl.ds(at, row_count), :] = value_block[...]
    unusable = jnp.where(mask[...][None, :] > 0, 0.0, -1e30)
    attended[...] = jnp.zeros_like(attended)
    for start in range(0, HEADS, together):
        heads = []
        for h in range(start, start + together):
            first, last = h * head_size, (h + 1) * head_size
            lo, hi = first // 128 * 128, -(-last // 128) * 128
            lanes = lax.broadcasted_iota(jnp.int32, (1, hi - lo), 1) + lo
            heads.append((h, lo, hi, (lanes >= first) & (lanes < last)))
        scores = [
            lax.dot_general(
                jnp.where(inside, queries[:, lo:hi], jnp.zeros((), jnp.bfloat16)),
                keys[:, lo:hi],
                (((1,), (1,)), ((), ())),
                preferred_element_type=jnp.float32,
            )
            for _, lo, hi, inside in heads
        ]
        for j in range(2):
            loads[2 * (start // together) + j].wait()
        weights, totals = [], []
        for (h, _, _, _), score in zip(heads, scores):
            score = score + bias[h].astype(jnp.float32) + unusable
            weight = jnp.exp(score - jnp.max(score, axis=1, keepdims=True))
            totals.append(jnp.sum(weight, axis=1, keepdims=True))
            weights.append(weight.astype(jnp.bfloat16))
        for (_, lo, hi, inside), weight, total in zip(heads, weights, totals):
            mixture = jnp.dot(weight, values[:, lo:hi], preferred_element_type=jnp.float32)
            attended[:, lo:hi] += jnp.where(inside, mixture / total, 0.0)
    for copy in later:
        copy.wait()
    stream = x_rows[...].astype(jnp.float32) + jnp.dot(
        attended[...].astype(jnp.bfloat16), w_o_here[...], preferred_element_type=jnp.float32
    )
    stream_ref[...] = stream
    normed_ff = rms_norm(stream, gain_ff[...][None, :]).astype(jnp.bfloat16)
    normed_ff_ref[...] = jnp.dot(
        normed_ff, order_here[...], preferred_element_type=jnp.float32
    ).astype(jnp.bfloat16)


def transition_kernel(
    own, other, stream, here, left, right, far_0, far_1, keep_ref, send_ref, weights, extras, arrived
):
    c, x = lax.axis_index("c"), lax.axis_index("x")
    half = own.shape[0] // 2
    width = own.shape[1]
    parts = [(block.at[i], across, i) for block, across in ((here, 0), (left, 3), (right, 1)) for i in range(2)]
    parts += [(far_0.at[0], 2, 0), (far_1.at[0], 2, 1)]
    copies = []
    for k, (part, across, i) in enumerate(parts):
        e = lax.rem(x + across, NX) * 2 + i
        copies.append(pltpu.make_async_copy(part.at[:GROUP], weights.at[e], arrived.at[2 * k]))
        copies.append(pltpu.make_async_copy(part.at[GROUP:], extras.at[e], arrived.at[2 * k + 1]))
    for copy in copies:
        copy.start()
    rows = jnp.concatenate([own[...], other[...]], axis=0)
    for copy in copies:
        copy.wait()

    def plain(tiles):
        return tiles.astype(jnp.float32).reshape(-1, width).astype(jnp.bfloat16)

    gate = jnp.dot(rows, weights[0:3].reshape(width, width), preferred_element_type=jnp.float32)
    up = jnp.dot(rows, weights[3:6].reshape(width, width), preferred_element_type=jnp.float32)
    out_row, in_row = iotas((GROUP * TILE, GROUP * TILE))
    onehot = in_row == out_row % TILE * GROUP + out_row // TILE
    last = reorder(onehot, plain(extras[...])).reshape(GROUP, 1, TILE, width)
    first = [weights[e].astype(jnp.float32).reshape(GROUP, 1, TILE, width) for e in (6, 7)]
    down = jnp.concatenate([*first, last], axis=1).reshape(width, width).astype(jnp.bfloat16)
    hidden = (gate / (1.0 + jnp.exp(-gate)) * up).astype(jnp.bfloat16)
    update = lax.dot_general(
        hidden, down, (((1,), (1,)), ((), ())), preferred_element_type=jnp.float32
    )
    keep_ref[c] = update[:half] + stream[:half]
    send_ref[c] = (update[half : 2 * half] + stream[half:]).astype(jnp.bfloat16)
    send_ref[1 - c] = update[2 * half : 3 * half].astype(jnp.bfloat16)
    keep_ref[1 - c] = update[3 * half :]


def swap_cores(value):
    return lax.ppermute(value, "c", [(0, 1), (1, 0)])


def others(value, axis, size):
    return [
        lax.ppermute(value, axis, [(i, (i + k) % size) for i in range(size)]) for k in range(1, size)
    ]


def kernel(f, name, specs, args, shapes, limit=8, scratch=(), out_spec=None, wait=1):
    def whole(shape):
        return pl.BlockSpec(shape, lambda i: (0,) * len(shape))

    specs = [whole(a.shape) if s is None else s for s, a in zip(specs, args, strict=True)]
    outs = tuple(jax.ShapeDtypeStruct(shape, dtype) for shape, dtype in shapes)
    return pl.pallas_call(
        f,
        grid=(1,),
        out_shape=outs,
        in_specs=specs,
        out_specs=tuple(out_spec or whole(o.shape) for o in outs),
        scratch_shapes=scratch,
        compiler_params=pltpu.CompilerParams(vmem_limit_bytes=limit * MIB),
        cost_estimate=pl.CostEstimate(
            flops=int(wait * MICROSECOND), bytes_accessed=0, transcendentals=0
        ),
        name=name,
    )(*args)


def body(states, ancestors, pair_bias, key_mask, gain_attn, w_qkv, w_o, gain_ff, w_in, w_out):
    part_count, block_rows, width = states.shape
    rows = block_rows * NC
    half = width // 2
    both = 2 * PIECE
    depth = w_out.shape[0]
    bf16, f32 = jnp.bfloat16, jnp.float32
    order_in = input_order(width)

    bias_other = swap_cores(pair_bias)
    (pieces,) = kernel(
        spread_kernel,
        "spread",
        [SMEM, None, None, None],
        (ancestors, states, w_in, w_out),
        [((GROUP // 2, 2, both, width + 128), bf16)],
        limit=56,
        scratch=[pltpu.VMEM((3 * depth, width), f32)],
    )
    pieces = lax.all_to_all(pieces.reshape(GROUP, both, width + 128), PARTICLE, 0, 0)
    come, piece, onehot = kernel(
        unpack_kernel,
        "unpack",
        [None],
        (pieces,),
        [
            ((GROUP * both, half), bf16),
            ((GROUP * (TILE + 1), half), bf16),
            ((GROUP * both, GROUP * both), bf16),
        ],
    )
    (picked,) = kernel(
        pick_kernel,
        "pick",
        [None, None],
        (onehot, come),
        [((GROUP, both, half), bf16)],
        limit=40,
        wait=1,
    )
    ring = [piece] + others(piece, "y", NY)
    (column,) = kernel(
        column_kernel,
        "column",
        [None] * NY,
        ring,
        [((2, GROUP * (TILE + 1), width), bf16)],
    )
    forward, back = ([(i, (i + k) % NX) for i in range(NX)] for k in (1, -1))
    left, right = lax.ppermute(column, "x", forward), lax.ppermute(column, "x", back)

    mine = lax.all_to_all(picked, PARTICLE, 0, 0)
    x_rows, normed = kernel(
        own_kernel,
        "own",
        [None, None, None, ANY],
        (mine, swap_cores(mine), gain_attn, bias_other),
        [((rows, width), bf16)] * 2,
    )
    queries, *own = kernel(
        project_kernel, "project", [None, VMEM], (normed, w_qkv), [((rows, width), bf16)] * 3
    )
    blocks = others(normed, "y", NY)
    made = [
        kernel(other_kernel, "other", [None, VMEM], (block, w_qkv), [((rows, width), bf16)] * 2)
        for block in blocks[1:]
    ]
    left_half, right_half = kernel(
        halves_kernel,
        "halves",
        [ANY] * 3,
        (left, right, made[0][0]),
        [((1,) + column.shape[1:], bf16)] * 2,
        out_spec=ANY,
        scratch=[pltpu.SemaphoreType.DMA((2,))],
    )
    first = kernel(
        other_kernel,
        "other",
        [None, VMEM, ANY, ANY],
        (blocks[0], w_qkv, left_half, right_half),
        [((rows, width), bf16)] * 2,
    )
    made = [own, first] + made
    far = [lax.ppermute(left_half, "x", forward), lax.ppermute(right_half, "x", back)]
    stream, normed_ff = kernel(
        attention_kernel,
        "attention",
        [None] * 10 + [ANY, ANY, None, ANY, None] + [ANY] * 3,
        (
            *[k for k, _ in made], *[v for _, v in made], queries, x_rows, pair_bias, bias_other,
            key_mask, w_o, gain_ff, order_in, left_half, right_half,
        ),
        [((rows, width), f32), ((rows, width), bf16)],
        limit=16,
        wait=4,
        scratch=[
            pltpu.VMEM((rows * NY, width), bf16),
            pltpu.VMEM((rows * NY, width), bf16),
            pltpu.VMEM((rows, width), f32),
            pltpu.VMEM((HEADS, rows, rows * NY), bf16),
            pltpu.VMEM((width, width), bf16),
            pltpu.VMEM((width, width), bf16),
            pltpu.SemaphoreType.DMA((6,)),
        ],
    )
    keep, send = kernel(
        transition_kernel,
        "transition",
        [None] * 3 + [ANY] * 5,
        (
            normed_ff, swap_cores(normed_ff), stream,
            *(w.reshape(w.shape[0], -1, TILE, width) for w in (column, left, right, *far)),
        ),
        [((part_count, block_rows, width), t) for t in (f32, bf16)],
        limit=16,
        scratch=[
            pltpu.VMEM((TILES, GROUP, TILE, width), bf16),
            pltpu.VMEM((TILES, GROUP // TILE, TILE, width), bf16),
            pltpu.SemaphoreType.DMA((16,)),
        ],
    )
    return (keep + swap_cores(send)).astype(bf16)


def solution(mesh):
    fine = Mesh(mesh.devices.reshape(NX, NZ, NY, NC), ("x", "z", "y", "c"))
    token = ("y", "c")
    placed = (
        P(PARTICLE, token, None),
        P(PARTICLE),
        P(None, token, None),
        P(),
        P(),
        P(),
        P(),
        P(),
        P(None, PARTICLE, None),
        P(PARTICLE, None),
    )
    return jax.shard_map(
        body, mesh=fine, in_specs=placed, out_specs=P(PARTICLE, token, None), check_vma=False
    )
```

```python
import math

import jax
import jax.numpy as jnp
import numpy as np
from jax import lax
from jax.experimental import pallas as pl
from jax.experimental.pallas import tpu as pltpu
from jax.sharding import Mesh
from jax.sharding import PartitionSpec as P

NX, NZ, NY, NC = 4, 8, 4, 2
GROUP = NX * NZ
PARTICLE = ("x", "z")
HEADS = 16
EPS = 1e-05
PIECE = 4
TILE = 8
TILES = 8
MIB = 2**20
MICROSECOND = 10**9
ANY = pl.BlockSpec(memory_space=pl.ANY)
VMEM = pl.BlockSpec(memory_space=pltpu.VMEM)
SMEM = pl.BlockSpec(memory_space=pltpu.SMEM)


def rms_norm(stream, gain_vec):
    return stream * lax.rsqrt(jnp.mean(stream * stream, axis=-1, keepdims=True) + EPS) * gain_vec


def iotas(shape):
    return lax.broadcasted_iota(jnp.int32, shape, 0), lax.broadcasted_iota(jnp.int32, shape, 1)


def reorder(onehot, values):
    return jnp.dot(onehot.astype(jnp.bfloat16), values, preferred_element_type=jnp.float32)


def input_order(width):
    depth = width // GROUP
    tile, source, row = np.meshgrid(np.arange(3), np.arange(GROUP), np.arange(TILE), indexing="ij")
    return np.eye(width, dtype=jnp.bfloat16)[:, (source * depth + tile * TILE + row).reshape(-1)]


def spread_kernel(ancestors, states, w_in, w_out, out_ref, local):
    y, c = lax.axis_index("y"), lax.axis_index("c")
    part_count, rows, width = states.shape
    half = width // 2
    both = 2 * PIECE
    out_row, in_row = iotas((part_count * rows, part_count * rows))
    group, part, row = out_row // both, out_row // PIECE % 2, out_row % PIECE
    onehot = in_row == part * rows + group * PIECE + row
    moved = reorder(onehot, states[...].reshape(part_count * rows, width))
    for h in range(2):
        out_ref[:, h, :, :half] = (
            moved[:, h * half : (h + 1) * half].reshape(-1, both, half).astype(jnp.bfloat16)
        )
    depth = w_out.shape[0]
    mine = pl.ds(pl.multiple_of(c * width, 128), width)
    local[: 2 * depth] = w_in[:, :, mine].astype(jnp.float32).reshape(2 * depth, width)
    local[2 * depth :] = w_out[:, mine].astype(jnp.float32)
    lanes = pl.ds(pl.multiple_of(lax.rem(y, 2) * half, 128), half)
    tile_row = lax.broadcasted_iota(jnp.int32, (both, 128), 0)
    names = jnp.where(tile_row == 3, ancestors[0], ancestors[1]).astype(jnp.float32)
    groups = GROUP // NX // 2
    for x in range(NX):
        e = 2 * x + y // 2
        tile = local[pl.ds(pl.multiple_of(e * TILE, TILE), TILE), lanes]
        extra = local[pl.ds(TILES * TILE + e, 1), lanes]
        last = names
        for i in range(3):
            last = jnp.where(tile_row == i, extra[:, i * 128 : (i + 1) * 128], last)
        at = slice(x * groups, (x + 1) * groups)
        shape = (groups, 2, both)
        out_ref[at, :, :, half:width] = jnp.broadcast_to(tile.astype(jnp.bfloat16), shape + (half,))
        out_ref[at, :, :, width:] = jnp.broadcast_to(last.astype(jnp.bfloat16), shape + (128,))


def unpack_kernel(pieces, states_ref, weights_ref, onehot_ref):
    half = states_ref.shape[1]
    width = 2 * half
    rows = pieces[...].astype(jnp.float32).reshape(-1, width + 128)
    count = rows.shape[0]
    states_ref[...] = rows[:, :half].astype(jnp.bfloat16)
    last = rows[:, width:].astype(jnp.bfloat16)
    weights_ref[:count] = rows[:, half:width].astype(jnp.bfloat16)
    out_row, in_row = iotas((GROUP, count))
    for i in range(3):
        extra = reorder(in_row == out_row * TILE + i, last).astype(jnp.bfloat16)
        weights_ref[count:, i * 128 : (i + 1) * 128] = extra
    out_row, in_row = iotas((count, count))
    part = lax.rem(out_row // PIECE + lax.axis_index("c"), 2)
    names = reorder(in_row == out_row // TILE * TILE + 3 + part, last)[:, :1]
    onehot = in_row == names.astype(jnp.int32) * PIECE + out_row % PIECE
    onehot_ref[...] = onehot.astype(jnp.bfloat16)


def pick_kernel(onehot, states, picked_ref):
    picked = reorder(onehot[...], states[...])
    picked_ref[...] = picked.reshape(picked_ref.shape).astype(jnp.bfloat16)


def column_kernel(w0, w1, w2, w3, out_ref):
    half = w0.shape[1]
    for k, block in enumerate((w0, w1, w2, w3)):
        y = lax.rem(lax.axis_index("y") + (NY - k), NY)
        lanes = pl.ds(pl.multiple_of(lax.rem(y, 2) * half, 128), half)
        out_ref[y // 2, :, lanes] = block[...]


def assemble(pieces, part, width):
    both = 2 * PIECE
    half = width // 2
    count = pieces.shape[0] // 2 * both
    out_row, in_row = iotas((count // 2, count))
    onehot = in_row == out_row // PIECE * both + part * PIECE + out_row % PIECE
    sides = []
    for h in range(2):
        values = pieces[:, :, :].reshape(-1, 2, both, half)[:, h]
        values = values.astype(jnp.float32).reshape(count, half).astype(jnp.bfloat16)
        sides.append(reorder(onehot, values))
    return jnp.concatenate(sides, axis=1)


def chip_rows(mine, theirs, width):
    return jnp.concatenate([assemble(mine, 0, width), assemble(theirs, 1, width)], axis=0)


def store_rows(ref, values):
    c = lax.axis_index("c")
    half = values.shape[0] // 2
    for slot, at in ((c, 0), (1 - c, half)):
        ref[pl.ds(pl.multiple_of(slot * half, half), half), :] = values[at : at + half].astype(ref.dtype)


def own_kernel(mine, theirs, gain, _bias, x_ref, normed_ref):
    rows = chip_rows(mine, theirs, x_ref.shape[1])
    x_ref[...] = rows.astype(jnp.bfloat16)
    store_rows(normed_ref, rms_norm(rows, gain[...][None, :]))


def project_kernel(normed, w_qkv, queries_ref, keys_ref, values_ref):
    width = keys_ref.shape[1]
    projected = jnp.dot(normed[...], w_qkv[...], preferred_element_type=jnp.float32)
    scale = 1.0 / math.sqrt(width // HEADS)
    store_rows(queries_ref, projected[:, :width] * scale)
    keys_ref[...] = projected[:, width : 2 * width].astype(jnp.bfloat16)
    values_ref[...] = projected[:, 2 * width :].astype(jnp.bfloat16)


def other_kernel(normed, w_qkv, *refs):
    keys_ref, values_ref = refs[-2:]
    width = keys_ref.shape[1]
    projected = jnp.dot(normed[...], w_qkv[:, width:], preferred_element_type=jnp.float32)
    keys_ref[...] = projected[:, :width].astype(jnp.bfloat16)
    values_ref[...] = projected[:, width:].astype(jnp.bfloat16)


def halves_kernel(left, right, _after, left_ref, right_ref, sent):
    copies = [
        pltpu.make_async_copy(left.at[:1], left_ref, sent.at[0]),
        pltpu.make_async_copy(right.at[1:], right_ref, sent.at[1]),
    ]
    for copy in copies:
        copy.start()
    for copy in copies:
        copy.wait()


def attention_kernel(
    k0, k1, k2, k3, v0, v1, v2, v3, queries, x_rows, bias_own, bias_other, mask, w_o, gain_ff, order,
    _left, _right, stream_ref, normed_ff_ref, keys, values, attended, bias, w_o_here, order_here, loaded,
):
    y = lax.axis_index("y")
    row_count, width = queries.shape
    half = row_count // 2
    head_size = width // HEADS
    together = 8
    loads = []
    for i in range(HEADS // together):
        part = pl.ds(i * together, together)
        for j, source in enumerate((bias_own, bias_other)):
            at = pl.ds(j * half, half)
            loads.append(
                pltpu.make_async_copy(source.at[part], bias.at[part, at], loaded.at[2 * i + j])
            )
    later = [
        pltpu.make_async_copy(w_o, w_o_here, loaded.at[len(loads)]),
        pltpu.make_async_copy(order, order_here, loaded.at[len(loads) + 1]),
    ]
    for copy in loads + later:
        copy.start()
    for k, (key_block, value_block) in enumerate(((k0, v0), (k1, v1), (k2, v2), (k3, v3))):
        at = pl.multiple_of(lax.rem(y + (NY - k), NY) * row_count, row_count)
        keys[pl.ds(at, row_count), :] = key_block[...]
        values[pl.ds(at, row_count), :] = value_block[...]
    unusable = jnp.where(mask[...][None, :] > 0, 0.0, -1e30)
    attended[...] = jnp.zeros_like(attended)
    for start in range(0, HEADS, together):
        heads = []
        for h in range(start, start + together):
            first, last = h * head_size, (h + 1) * head_size
            lo, hi = first // 128 * 128, -(-last // 128) * 128
            lanes = lax.broadcasted_iota(jnp.int32, (1, hi - lo), 1) + lo
            heads.append((h, lo, hi, (lanes >= first) & (lanes < last)))
        scores = [
            lax.dot_general(
                jnp.where(inside, queries[:, lo:hi], jnp.zeros((), jnp.bfloat16)),
                keys[:, lo:hi],
                (((1,), (1,)), ((), ())),
                preferred_element_type=jnp.float32,
            )
            for _, lo, hi, inside in heads
        ]
        for j in range(2):
            loads[2 * (start // together) + j].wait()
        weights, totals = [], []
        for (h, _, _, _), score in zip(heads, scores):
            score = score + bias[h].astype(jnp.float32) + unusable
            weight = jnp.exp(score - jnp.max(score, axis=1, keepdims=True))
            totals.append(jnp.sum(weight, axis=1, keepdims=True))
            weights.append(weight.astype(jnp.bfloat16))
        for (_, lo, hi, inside), weight, total in zip(heads, weights, totals):
            mixture = jnp.dot(weight, values[:, lo:hi], preferred_element_type=jnp.float32)
            attended[:, lo:hi] += jnp.where(inside, mixture / total, 0.0)
    for copy in later:
        copy.wait()
    stream = x_rows[...].astype(jnp.float32) + jnp.dot(
        attended[...].astype(jnp.bfloat16), w_o_here[...], preferred_element_type=jnp.float32
    )
    stream_ref[...] = stream
    normed_ff = rms_norm(stream, gain_ff[...][None, :]).astype(jnp.bfloat16)
    normed_ff_ref[...] = jnp.dot(
        normed_ff, order_here[...], preferred_element_type=jnp.float32
    ).astype(jnp.bfloat16)


def transition_kernel(
    own, other, stream, here, left, right, far_0, far_1, keep_ref, send_ref, weights, extras, arrived
):
    c, x = lax.axis_index("c"), lax.axis_index("x")
    half = own.shape[0] // 2
    width = own.shape[1]
    columns = (
        (here.at[0], here.at[1]),
        (right.at[0], right.at[1]),
        (far_0.at[0], far_1.at[0]),
        (left.at[0], left.at[1]),
    )

    def copies(source, column):
        return [
            copy
            for i, part in enumerate(column)
            for copy in (
                pltpu.make_async_copy(
                    part.at[:GROUP], weights.at[2 * source + i], arrived.at[4 * source + 2 * i]
                ),
                pltpu.make_async_copy(
                    part.at[GROUP:], extras.at[2 * source + i], arrived.at[4 * source + 2 * i + 1]
                ),
            )
        ]

    def wait(source):
        for copy in copies(source, columns[0]):
            copy.wait()

    for source in range(NX):
        for across, column in enumerate(columns):

            @pl.when(lax.rem(x + across, NX) == source)
            def _():
                for copy in copies(source, column):
                    copy.start()

    rows = jnp.concatenate([own[...], other[...]], axis=0)
    wait(0)
    wait(1)

    def plain(tiles):
        return tiles.astype(jnp.float32).reshape(-1, width).astype(jnp.bfloat16)

    gate = jnp.dot(rows, weights[0:3].reshape(width, width), preferred_element_type=jnp.float32)
    wait(2)
    up = jnp.dot(rows, weights[3:6].reshape(width, width), preferred_element_type=jnp.float32)
    wait(3)
    out_row, in_row = iotas((GROUP * TILE, GROUP * TILE))
    onehot = in_row == out_row % TILE * GROUP + out_row // TILE
    last = reorder(onehot, plain(extras[...])).reshape(GROUP, 1, TILE, width)
    first = [weights[e].astype(jnp.float32).reshape(GROUP, 1, TILE, width) for e in (6, 7)]
    down = jnp.concatenate([*first, last], axis=1).reshape(width, width).astype(jnp.bfloat16)
    hidden = (gate / (1.0 + jnp.exp(-gate)) * up).astype(jnp.bfloat16)
    update = lax.dot_general(
        hidden, down, (((1,), (1,)), ((), ())), preferred_element_type=jnp.float32
    )
    keep_ref[c] = update[:half] + stream[:half]
    send_ref[c] = (update[half : 2 * half] + stream[half:]).astype(jnp.bfloat16)
    send_ref[1 - c] = update[2 * half : 3 * half].astype(jnp.bfloat16)
    keep_ref[1 - c] = update[3 * half :]


def swap_cores(value):
    return lax.ppermute(value, "c", [(0, 1), (1, 0)])


def others(value, axis, size):
    return [
        lax.ppermute(value, axis, [(i, (i + k) % size) for i in range(size)]) for k in range(1, size)
    ]


def kernel(f, name, specs, args, shapes, limit=8, scratch=(), out_spec=None, wait=1):
    def whole(shape):
        return pl.BlockSpec(shape, lambda i: (0,) * len(shape))

    specs = [whole(a.shape) if s is None else s for s, a in zip(specs, args, strict=True)]
    outs = tuple(jax.ShapeDtypeStruct(shape, dtype) for shape, dtype in shapes)
    return pl.pallas_call(
        f,
        grid=(1,),
        out_shape=outs,
        in_specs=specs,
        out_specs=tuple(out_spec or whole(o.shape) for o in outs),
        scratch_shapes=scratch,
        compiler_params=pltpu.CompilerParams(vmem_limit_bytes=limit * MIB),
        cost_estimate=pl.CostEstimate(
            flops=int(wait * MICROSECOND), bytes_accessed=0, transcendentals=0
        ),
        name=name,
    )(*args)


def body(states, ancestors, pair_bias, key_mask, gain_attn, w_qkv, w_o, gain_ff, w_in, w_out):
    part_count, block_rows, width = states.shape
    rows = block_rows * NC
    half = width // 2
    both = 2 * PIECE
    depth = w_out.shape[0]
    bf16, f32 = jnp.bfloat16, jnp.float32
    order_in = input_order(width)

    bias_other = swap_cores(pair_bias)
    (pieces,) = kernel(
        spread_kernel,
        "spread",
        [SMEM, None, None, None],
        (ancestors, states, w_in, w_out),
        [((GROUP // 2, 2, both, width + 128), bf16)],
        limit=56,
        scratch=[pltpu.VMEM((3 * depth, width), f32)],
    )
    pieces = lax.all_to_all(pieces.reshape(GROUP, both, width + 128), PARTICLE, 0, 0)
    come, piece, onehot = kernel(
        unpack_kernel,
        "unpack",
        [None],
        (pieces,),
        [
            ((GROUP * both, half), bf16),
            ((GROUP * (TILE + 1), half), bf16),
            ((GROUP * both, GROUP * both), bf16),
        ],
    )
    (picked,) = kernel(
        pick_kernel,
        "pick",
        [None, None],
        (onehot, come),
        [((GROUP, both, half), bf16)],
        limit=40,
        wait=1,
    )
    ring = [piece] + others(piece, "y", NY)
    (column,) = kernel(
        column_kernel,
        "column",
        [None] * NY,
        ring,
        [((2, GROUP * (TILE + 1), width), bf16)],
    )
    forward, back = ([(i, (i + k) % NX) for i in range(NX)] for k in (1, -1))
    left, right = lax.ppermute(column, "x", forward), lax.ppermute(column, "x", back)

    mine = lax.all_to_all(picked, PARTICLE, 0, 0)
    x_rows, normed = kernel(
        own_kernel,
        "own",
        [None, None, None, ANY],
        (mine, swap_cores(mine), gain_attn, bias_other),
        [((rows, width), bf16)] * 2,
    )
    queries, *own = kernel(
        project_kernel, "project", [None, VMEM], (normed, w_qkv), [((rows, width), bf16)] * 3
    )
    blocks = others(normed, "y", NY)
    made = [
        kernel(other_kernel, "other", [None, VMEM], (block, w_qkv), [((rows, width), bf16)] * 2)
        for block in blocks[1:]
    ]
    left_half, right_half = kernel(
        halves_kernel,
        "halves",
        [ANY] * 3,
        (left, right, made[0][0]),
        [((1,) + column.shape[1:], bf16)] * 2,
        out_spec=ANY,
        scratch=[pltpu.SemaphoreType.DMA((2,))],
    )
    first = kernel(
        other_kernel,
        "other",
        [None, VMEM, ANY, ANY],
        (blocks[0], w_qkv, left_half, right_half),
        [((rows, width), bf16)] * 2,
    )
    made = [own, first] + made
    far = [lax.ppermute(left_half, "x", forward), lax.ppermute(right_half, "x", back)]
    stream, normed_ff = kernel(
        attention_kernel,
        "attention",
        [None] * 10 + [ANY, ANY, None, ANY, None] + [ANY] * 3,
        (
            *[k for k, _ in made], *[v for _, v in made], queries, x_rows, pair_bias, bias_other,
            key_mask, w_o, gain_ff, order_in, left_half, right_half,
        ),
        [((rows, width), f32), ((rows, width), bf16)],
        limit=16,
        wait=4,
        scratch=[
            pltpu.VMEM((rows * NY, width), bf16),
            pltpu.VMEM((rows * NY, width), bf16),
            pltpu.VMEM((rows, width), f32),
            pltpu.VMEM((HEADS, rows, rows * NY), bf16),
            pltpu.VMEM((width, width), bf16),
            pltpu.VMEM((width, width), bf16),
            pltpu.SemaphoreType.DMA((6,)),
        ],
    )
    keep, send = kernel(
        transition_kernel,
        "transition",
        [None] * 3 + [ANY] * 5,
        (
            normed_ff, swap_cores(normed_ff), stream,
            *(w.reshape(w.shape[0], -1, TILE, width) for w in (column, left, right, *far)),
        ),
        [((part_count, block_rows, width), t) for t in (f32, bf16)],
        limit=16,
        scratch=[
            pltpu.VMEM((TILES, GROUP, TILE, width), bf16),
            pltpu.VMEM((TILES, GROUP // TILE, TILE, width), bf16),
            pltpu.SemaphoreType.DMA((16,)),
        ],
    )
    return (keep + swap_cores(send)).astype(bf16)


def solution(mesh):
    fine = Mesh(mesh.devices.reshape(NX, NZ, NY, NC), ("x", "z", "y", "c"))
    token = ("y", "c")
    placed = (
        P(PARTICLE, token, None),
        P(PARTICLE),
        P(None, token, None),
        P(),
        P(),
        P(),
        P(),
        P(),
        P(None, PARTICLE, None),
        P(PARTICLE, None),
    )
    return jax.shard_map(
        body, mesh=fine, in_specs=placed, out_specs=P(PARTICLE, token, None), check_vma=False
    )
```

```python
import math

import jax
import jax.numpy as jnp
import numpy as np
from jax import lax
from jax.experimental import pallas as pl
from jax.experimental.pallas import tpu as pltpu
from jax.sharding import Mesh
from jax.sharding import PartitionSpec as P

NX, NZ, NY, NC = 4, 8, 4, 2
GROUP = NX * NZ
PARTICLE = ("x", "z")
HEADS = 16
EPS = 1e-05
PIECE = 4
TILE = 8
TILES = 8
MIB = 2**20
MICROSECOND = 10**9
ANY = pl.BlockSpec(memory_space=pl.ANY)
VMEM = pl.BlockSpec(memory_space=pltpu.VMEM)
SMEM = pl.BlockSpec(memory_space=pltpu.SMEM)


def rms_norm(stream, gain_vec):
    return stream * lax.rsqrt(jnp.mean(stream * stream, axis=-1, keepdims=True) + EPS) * gain_vec


def iotas(shape):
    return lax.broadcasted_iota(jnp.int32, shape, 0), lax.broadcasted_iota(jnp.int32, shape, 1)


def reorder(onehot, values):
    return jnp.dot(onehot.astype(jnp.bfloat16), values, preferred_element_type=jnp.float32)


def input_order(width):
    depth = width // GROUP
    tile, source, row = np.meshgrid(np.arange(3), np.arange(GROUP), np.arange(TILE), indexing="ij")
    return np.eye(width, dtype=jnp.bfloat16)[:, (source * depth + tile * TILE + row).reshape(-1)]


def spread_kernel(ancestors, states, w_in, w_out, out_ref, local):
    y, c = lax.axis_index("y"), lax.axis_index("c")
    part_count, rows, width = states.shape
    half = width // 2
    both = 2 * PIECE
    out_row, in_row = iotas((part_count * rows, part_count * rows))
    group, part, row = out_row // both, out_row // PIECE % 2, out_row % PIECE
    onehot = in_row == part * rows + group * PIECE + row
    moved = reorder(onehot, states[...].reshape(part_count * rows, width))
    for h in range(2):
        out_ref[:, h, :, :half] = (
            moved[:, h * half : (h + 1) * half].reshape(-1, both, half).astype(jnp.bfloat16)
        )
    depth = w_out.shape[0]
    mine = pl.ds(pl.multiple_of(c * width, 128), width)
    local[: 2 * depth] = w_in[:, :, mine].astype(jnp.float32).reshape(2 * depth, width)
    local[2 * depth :] = w_out[:, mine].astype(jnp.float32)
    lanes = pl.ds(pl.multiple_of(lax.rem(y, 2) * half, 128), half)
    tile_row = lax.broadcasted_iota(jnp.int32, (both, 128), 0)
    names = jnp.where(tile_row == 3, ancestors[0], ancestors[1]).astype(jnp.float32)
    groups = GROUP // NX // 2
    for x in range(NX):
        e = 2 * x + y // 2
        tile = local[pl.ds(pl.multiple_of(e * TILE, TILE), TILE), lanes]
        extra = local[pl.ds(TILES * TILE + e, 1), lanes]
        last = names
        for i in range(3):
            last = jnp.where(tile_row == i, extra[:, i * 128 : (i + 1) * 128], last)
        at = slice(x * groups, (x + 1) * groups)
        shape = (groups, 2, both)
        out_ref[at, :, :, half:width] = jnp.broadcast_to(tile.astype(jnp.bfloat16), shape + (half,))
        out_ref[at, :, :, width:] = jnp.broadcast_to(last.astype(jnp.bfloat16), shape + (128,))


def unpack_kernel(pieces, states_ref, weights_ref, onehot_ref):
    half = states_ref.shape[1]
    width = 2 * half
    rows = pieces[...].astype(jnp.float32).reshape(-1, width + 128)
    count = rows.shape[0]
    states_ref[...] = rows[:, :half].astype(jnp.bfloat16)
    last = rows[:, width:].astype(jnp.bfloat16)
    weights_ref[:count] = rows[:, half:width].astype(jnp.bfloat16)
    out_row, in_row = iotas((GROUP, count))
    for i in range(3):
        extra = reorder(in_row == out_row * TILE + i, last).astype(jnp.bfloat16)
        weights_ref[count:, i * 128 : (i + 1) * 128] = extra
    out_row, in_row = iotas((count, count))
    part = lax.rem(out_row // PIECE + lax.axis_index("c"), 2)
    names = reorder(in_row == out_row // TILE * TILE + 3 + part, last)[:, :1]
    onehot = in_row == names.astype(jnp.int32) * PIECE + out_row % PIECE
    onehot_ref[...] = onehot.astype(jnp.bfloat16)


def pick_kernel(onehot, states, picked_ref):
    picked = reorder(onehot[...], states[...])
    picked_ref[...] = picked.reshape(picked_ref.shape).astype(jnp.bfloat16)


def column_kernel(w0, w1, w2, w3, out_ref):
    half = w0.shape[1]
    for k, block in enumerate((w0, w1, w2, w3)):
        y = lax.rem(lax.axis_index("y") + (NY - k), NY)
        lanes = pl.ds(pl.multiple_of(lax.rem(y, 2) * half, 128), half)
        out_ref[y // 2, :, lanes] = block[...]


def assemble(pieces, part, width):
    both = 2 * PIECE
    half = width // 2
    count = pieces.shape[0] // 2 * both
    out_row, in_row = iotas((count // 2, count))
    onehot = in_row == out_row // PIECE * both + part * PIECE + out_row % PIECE
    sides = []
    for h in range(2):
        values = pieces[:, :, :].reshape(-1, 2, both, half)[:, h]
        values = values.astype(jnp.float32).reshape(count, half).astype(jnp.bfloat16)
        sides.append(reorder(onehot, values))
    return jnp.concatenate(sides, axis=1)


def chip_rows(mine, theirs, width):
    return jnp.concatenate([assemble(mine, 0, width), assemble(theirs, 1, width)], axis=0)


def store_rows(ref, values):
    c = lax.axis_index("c")
    half = values.shape[0] // 2
    for slot, at in ((c, 0), (1 - c, half)):
        ref[pl.ds(pl.multiple_of(slot * half, half), half), :] = values[at : at + half].astype(ref.dtype)


def own_kernel(mine, theirs, gain, _bias, x_ref, normed_ref):
    rows = chip_rows(mine, theirs, x_ref.shape[1])
    x_ref[...] = rows.astype(jnp.bfloat16)
    store_rows(normed_ref, rms_norm(rows, gain[...][None, :]))


def project_kernel(normed, w_qkv, queries_ref, keys_ref, values_ref):
    width = keys_ref.shape[1]
    projected = jnp.dot(normed[...], w_qkv[...], preferred_element_type=jnp.float32)
    scale = 1.0 / math.sqrt(width // HEADS)
    store_rows(queries_ref, projected[:, :width] * scale)
    keys_ref[...] = projected[:, width : 2 * width].astype(jnp.bfloat16)
    values_ref[...] = projected[:, 2 * width :].astype(jnp.bfloat16)


def other_kernel(normed, w_qkv, *refs):
    keys_ref, values_ref = refs[-2:]
    width = keys_ref.shape[1]
    projected = jnp.dot(normed[...], w_qkv[:, width:], preferred_element_type=jnp.float32)
    keys_ref[...] = projected[:, :width].astype(jnp.bfloat16)
    values_ref[...] = projected[:, width:].astype(jnp.bfloat16)


def halves_kernel(left, right, _after, left_ref, right_ref, sent):
    copies = [
        pltpu.make_async_copy(left.at[:1], left_ref, sent.at[0]),
        pltpu.make_async_copy(right.at[1:], right_ref, sent.at[1]),
    ]
    for copy in copies:
        copy.start()
    for copy in copies:
        copy.wait()


def attention_kernel(
    k0, k1, k2, k3, v0, v1, v2, v3, queries, x_rows, bias_own, bias_other, mask, w_o, gain_ff, order,
    _left, _right, stream_ref, normed_ff_ref, keys, values, attended, bias, w_o_here, order_here, loaded,
):
    y = lax.axis_index("y")
    row_count, width = queries.shape
    half = row_count // 2
    head_size = width // HEADS
    together = 8
    loads = []
    for i in range(HEADS // together):
        part = pl.ds(i * together, together)
        for j, source in enumerate((bias_own, bias_other)):
            at = pl.ds(j * half, half)
            loads.append(
                pltpu.make_async_copy(source.at[part], bias.at[part, at], loaded.at[2 * i + j])
            )
    later = [
        pltpu.make_async_copy(w_o, w_o_here, loaded.at[len(loads)]),
        pltpu.make_async_copy(order, order_here, loaded.at[len(loads) + 1]),
    ]
    for copy in loads + later:
        copy.start()
    for k, (key_block, value_block) in enumerate(((k0, v0), (k1, v1), (k2, v2), (k3, v3))):
        at = pl.multiple_of(lax.rem(y + (NY - k), NY) * row_count, row_count)
        keys[pl.ds(at, row_count), :] = key_block[...]
        values[pl.ds(at, row_count), :] = value_block[...]
    unusable = jnp.where(mask[...][None, :] > 0, 0.0, -1e30)
    attended[...] = jnp.zeros_like(attended)
    for start in range(0, HEADS, together):
        heads = []
        for h in range(start, start + together):
            first, last = h * head_size, (h + 1) * head_size
            lo, hi = first // 128 * 128, -(-last // 128) * 128
            lanes = lax.broadcasted_iota(jnp.int32, (1, hi - lo), 1) + lo
            heads.append((h, lo, hi, (lanes >= first) & (lanes < last)))
        scores = [
            lax.dot_general(
                jnp.where(inside, queries[:, lo:hi], jnp.zeros((), jnp.bfloat16)),
                keys[:, lo:hi],
                (((1,), (1,)), ((), ())),
                preferred_element_type=jnp.float32,
            )
            for _, lo, hi, inside in heads
        ]
        for j in range(2):
            loads[2 * (start // together) + j].wait()
        weights, totals = [], []
        for (h, _, _, _), score in zip(heads, scores):
            score = score + bias[h].astype(jnp.float32) + unusable
            weight = jnp.exp(score - jnp.max(score, axis=1, keepdims=True))
            totals.append(jnp.sum(weight, axis=1, keepdims=True))
            weights.append(weight.astype(jnp.bfloat16))
        for (_, lo, hi, inside), weight, total in zip(heads, weights, totals):
            mixture = jnp.dot(weight, values[:, lo:hi], preferred_element_type=jnp.float32)
            attended[:, lo:hi] += jnp.where(inside, mixture / total, 0.0)
    for copy in later:
        copy.wait()
    stream = x_rows[...].astype(jnp.float32) + jnp.dot(
        attended[...].astype(jnp.bfloat16), w_o_here[...], preferred_element_type=jnp.float32
    )
    stream_ref[...] = stream
    normed_ff = rms_norm(stream, gain_ff[...][None, :]).astype(jnp.bfloat16)
    normed_ff_ref[...] = jnp.dot(
        normed_ff, order_here[...], preferred_element_type=jnp.float32
    ).astype(jnp.bfloat16)


def transition_kernel(
    own, other, stream, here, left, right, far_0, far_1, keep_ref, send_ref, weights, extras, arrived
):
    c, x = lax.axis_index("c"), lax.axis_index("x")
    half = own.shape[0] // 2
    width = own.shape[1]
    parts = [(block.at[i], across, i) for block, across in ((here, 0), (left, 3), (right, 1)) for i in range(2)]
    parts += [(far_0.at[0], 2, 0), (far_1.at[0], 2, 1)]
    copies = []
    for k, (part, across, i) in enumerate(parts):
        e = lax.rem(x + across, NX) * 2 + i
        copies.append(pltpu.make_async_copy(part.at[:GROUP], weights.at[e], arrived.at[2 * k]))
        copies.append(pltpu.make_async_copy(part.at[GROUP:], extras.at[e], arrived.at[2 * k + 1]))
    for copy in copies:
        copy.start()
    rows = jnp.concatenate([own[...], other[...]], axis=0)
    for copy in copies:
        copy.wait()

    def plain(tiles):
        return tiles.astype(jnp.float32).reshape(-1, width).astype(jnp.bfloat16)

    gate = jnp.dot(rows, weights[0:3].reshape(width, width), preferred_element_type=jnp.float32)
    up = jnp.dot(rows, weights[3:6].reshape(width, width), preferred_element_type=jnp.float32)
    out_row, in_row = iotas((GROUP * TILE, GROUP * TILE))
    onehot = in_row == out_row % TILE * GROUP + out_row // TILE
    last = reorder(onehot, plain(extras[...])).reshape(GROUP, 1, TILE, width)
    first = [weights[e].astype(jnp.float32).reshape(GROUP, 1, TILE, width) for e in (6, 7)]
    down = jnp.concatenate([*first, last], axis=1).reshape(width, width).astype(jnp.bfloat16)
    hidden = (gate / (1.0 + jnp.exp(-gate)) * up).astype(jnp.bfloat16)
    update = lax.dot_general(
        hidden, down, (((1,), (1,)), ((), ())), preferred_element_type=jnp.float32
    )
    keep_ref[c] = update[:half] + stream[:half]
    send_ref[c] = (update[half : 2 * half] + stream[half:]).astype(jnp.bfloat16)
    send_ref[1 - c] = update[2 * half : 3 * half].astype(jnp.bfloat16)
    keep_ref[1 - c] = update[3 * half :]


def swap_cores(value):
    return lax.ppermute(value, "c", [(0, 1), (1, 0)])


def others(value, axis, size):
    return [
        lax.ppermute(value, axis, [(i, (i + k) % size) for i in range(size)]) for k in range(1, size)
    ]


def kernel(f, name, specs, args, shapes, limit=8, scratch=(), out_spec=None, wait=1):
    def whole(shape):
        return pl.BlockSpec(shape, lambda i: (0,) * len(shape))

    specs = [whole(a.shape) if s is None else s for s, a in zip(specs, args, strict=True)]
    outs = tuple(jax.ShapeDtypeStruct(shape, dtype) for shape, dtype in shapes)
    return pl.pallas_call(
        f,
        grid=(1,),
        out_shape=outs,
        in_specs=specs,
        out_specs=tuple(out_spec or whole(o.shape) for o in outs),
        scratch_shapes=scratch,
        compiler_params=pltpu.CompilerParams(vmem_limit_bytes=limit * MIB),
        cost_estimate=pl.CostEstimate(
            flops=int(wait * MICROSECOND), bytes_accessed=0, transcendentals=0
        ),
        name=name,
    )(*args)


def body(states, ancestors, pair_bias, key_mask, gain_attn, w_qkv, w_o, gain_ff, w_in, w_out):
    part_count, block_rows, width = states.shape
    rows = block_rows * NC
    half = width // 2
    both = 2 * PIECE
    depth = w_out.shape[0]
    bf16, f32 = jnp.bfloat16, jnp.float32
    order_in = input_order(width)

    bias_other = swap_cores(pair_bias)
    (pieces,) = kernel(
        spread_kernel,
        "spread",
        [SMEM, None, None, None],
        (ancestors, states, w_in, w_out),
        [((GROUP // 2, 2, both, width + 128), bf16)],
        limit=56,
        scratch=[pltpu.VMEM((3 * depth, width), f32)],
    )
    pieces = lax.all_to_all(pieces.reshape(GROUP, both, width + 128), PARTICLE, 0, 0)
    come, piece, onehot = kernel(
        unpack_kernel,
        "unpack",
        [None],
        (pieces,),
        [
            ((GROUP * both, half), bf16),
            ((GROUP * (TILE + 1), half), bf16),
            ((GROUP * both, GROUP * both), bf16),
        ],
    )
    (picked,) = kernel(
        pick_kernel,
        "pick",
        [None, None],
        (onehot, come),
        [((GROUP, both, half), bf16)],
        limit=40,
        wait=1,
    )
    ring = [piece] + others(piece, "y", NY)
    (column,) = kernel(
        column_kernel,
        "column",
        [None] * NY,
        ring,
        [((2, GROUP * (TILE + 1), width), bf16)],
    )
    forward, back = ([(i, (i + k) % NX) for i in range(NX)] for k in (1, -1))
    left, right = lax.ppermute(column, "x", forward), lax.ppermute(column, "x", back)

    mine = lax.all_to_all(picked, PARTICLE, 0, 0)
    x_rows, normed = kernel(
        own_kernel,
        "own",
        [None, None, None, ANY],
        (mine, swap_cores(mine), gain_attn, bias_other),
        [((rows, width), bf16)] * 2,
    )
    queries, *own = kernel(
        project_kernel, "project", [None, VMEM], (normed, w_qkv), [((rows, width), bf16)] * 3
    )
    blocks = others(normed, "y", NY)
    made = [
        kernel(other_kernel, "other", [None, VMEM], (block, w_qkv), [((rows, width), bf16)] * 2)
        for block in blocks[1:]
    ]
    left_half, right_half = kernel(
        halves_kernel,
        "halves",
        [ANY] * 3,
        (left, right, made[1][0]),
        [((1,) + column.shape[1:], bf16)] * 2,
        out_spec=ANY,
        scratch=[pltpu.SemaphoreType.DMA((2,))],
    )
    first = kernel(
        other_kernel,
        "other",
        [None, VMEM, ANY, ANY],
        (blocks[0], w_qkv, left_half, right_half),
        [((rows, width), bf16)] * 2,
    )
    made = [own, first] + made
    far = [lax.ppermute(left_half, "x", forward), lax.ppermute(right_half, "x", back)]
    stream, normed_ff = kernel(
        attention_kernel,
        "attention",
        [None] * 10 + [ANY, ANY, None, ANY, None] + [ANY] * 3,
        (
            *[k for k, _ in made], *[v for _, v in made], queries, x_rows, pair_bias, bias_other,
            key_mask, w_o, gain_ff, order_in, left_half, right_half,
        ),
        [((rows, width), f32), ((rows, width), bf16)],
        limit=16,
        wait=4,
        scratch=[
            pltpu.VMEM((rows * NY, width), bf16),
            pltpu.VMEM((rows * NY, width), bf16),
            pltpu.VMEM((rows, width), f32),
            pltpu.VMEM((HEADS, rows, rows * NY), bf16),
            pltpu.VMEM((width, width), bf16),
            pltpu.VMEM((width, width), bf16),
            pltpu.SemaphoreType.DMA((6,)),
        ],
    )
    keep, send = kernel(
        transition_kernel,
        "transition",
        [None] * 3 + [ANY] * 5,
        (
            normed_ff, swap_cores(normed_ff), stream,
            *(w.reshape(w.shape[0], -1, TILE, width) for w in (column, left, right, *far)),
        ),
        [((part_count, block_rows, width), t) for t in (f32, bf16)],
        limit=16,
        scratch=[
            pltpu.VMEM((TILES, GROUP, TILE, width), bf16),
            pltpu.VMEM((TILES, GROUP // TILE, TILE, width), bf16),
            pltpu.SemaphoreType.DMA((16,)),
        ],
    )
    return (keep + swap_cores(send)).astype(bf16)


def solution(mesh):
    fine = Mesh(mesh.devices.reshape(NX, NZ, NY, NC), ("x", "z", "y", "c"))
    token = ("y", "c")
    placed = (
        P(PARTICLE, token, None),
        P(PARTICLE),
        P(None, token, None),
        P(),
        P(),
        P(),
        P(),
        P(),
        P(None, PARTICLE, None),
        P(PARTICLE, None),
    )
    return jax.shard_map(
        body, mesh=fine, in_specs=placed, out_specs=P(PARTICLE, token, None), check_vma=False
    )
```
